32 devices in a mesh: section: 4 (over y, x), dp: 8 (over z, core).
Axes of the slice: x: 2, y: 2, z: 4, core: 2. Of those that a mesh axis runs over, the one named last changes fastest.
Arguments:
- acts: bfloat16 [8192, 768], P('dp'), may hold values from -6 to 6
- cotan: bfloat16 [8192, 768], P('dp'), may hold values from -6 to 6
- counts: int32 [64, 2], P('dp'), may hold values from 1 to 112, as said below
- weight_in: bfloat16 [4, 768, 3072], P('section'), may hold values from -0.3125 to 0.3125
- weight_out: bfloat16 [4, 3072, 768], P('section'), may hold values from -0.3125 to 0.3125
- ln_gain: float32 [4, 768], P('section'), may hold values from 0.5 to 1.5
- ln_bias: float32 [4, 768], P('section'), may hold values from -3 to 3
- gate_vec: float32 [4, 2, 768], P('section'), may hold values from -0.21875 to 0.21875
Outputs:
- section_outputs: bfloat16 [4, 8192, 768], P('section', 'dp')
- input_grads: bfloat16 [4, 8192, 768], P('section', 'dp')
- grad_weight_in: float32 [4, 768, 3072], P('section')
- grad_weight_out: float32 [4, 3072, 768], P('section')
- grad_ln_gain: float32 [4, 768], P('section')
- grad_ln_bias: float32 [4, 768], P('section')
- grad_gate_vec: float32 [4, 2, 768], P('section')
The draws below stay inside these ranges and needn't reach their ends.
Inputs may be any that keep to these rules, and one draw needn't show every extreme that they name: `counts`: every page has 1 to 16 live visual blocks and 1 to 112 live text blocks; some page has 16 and 112.
All inputs are finite; a program needn't handle non-finite values.
Results may differ from the reference program's by a relative error of at most 0.022.
Values may be sent and summed in bfloat16 or wider, within the bound.
No kernel may reach another device: no remote copies, remote signals or barrier semaphores. Data moves between devices by JAX's collectives and lax.ppermute only.
A program may use at most 128 MiB of HBM per device.

```python
import math
import jax
import jax.numpy as jnp
from jax import lax

D = 768
HEADS = 12
HEAD_DIM = 64
FF = 3072
VIS = 16
TXT = 112
PAGES = 64
TOKENS = 8192
N_SECTION = 4


def draw_counts(key, part):
    key = jax.random.fold_in(key, 7)
    key_visual, key_text = jax.random.split(key)
    raw_draw = jax.random.randint(key_visual, (PAGES,), 0, VIS + 1)
    vis_count = jnp.minimum(1 + raw_draw * raw_draw // VIS, VIS)
    text_count = jax.random.randint(key_text, (PAGES,), TXT // 4 + 1, TXT + 1)
    vis_count = vis_count.at[0].set(VIS)
    text_count = text_count.at[0].set(TXT)
    return jnp.stack([vis_count, text_count], axis=1).astype(jnp.int32)


def block_scale(stream_key, extent, cuts, least, largest):
    loudness, own = 1.0, jax.random.fold_in(stream_key, 6)
    for axis_at, parts in cuts:
        heights = jnp.exp(jax.random.uniform(jax.random.fold_in(own, axis_at), (parts,), jnp.float32, least / len(cuts), largest / len(cuts)))
        loudness = loudness * jnp.repeat(heights, extent[axis_at] // parts).reshape([-1 if axis == axis_at else 1 for axis in range(len(extent))])
    return loudness


def normal_values(own_key, dims, spread, limit, cuts=(), kind=jnp.bfloat16):
    gain = block_scale(own_key, dims, cuts, -0.22, 0.18) if cuts else 1.0
    drawn = jax.random.normal(own_key, dims, jnp.float32) * spread * gain
    return jnp.minimum(jnp.maximum(drawn, -limit), limit).astype(kind)


def setup_inputs(seed: int = 0) -> dict:
    key_list = jax.random.split(jax.random.key(seed), 9)
    return {
        "acts": normal_values(key_list[0], (TOKENS, D), 1.0, 6.0, ((0, 8),)),
        "cotan": normal_values(key_list[1], (TOKENS, D), 1.0, 6.0, ((0, 8),)),
        "counts": draw_counts(jax.random.fold_in(key_list[8], 71), 0),
        "weight_in": normal_values(key_list[3], (N_SECTION, D, FF), (D // 2) ** -0.5, 0.3125, ((0, 4),)),
        "weight_out": normal_values(key_list[4], (N_SECTION, FF, D), (D // 2) ** -0.5, 0.3125, ((0, 4),)),
        "ln_gain": jnp.clip(1.0 + 0.1 * jax.random.normal(key_list[5], (N_SECTION, D), jnp.float32), 0.5, 1.5),
        "ln_bias": normal_values(key_list[6], (N_SECTION, D), 0.5, 3.0, ((0, 4),), jnp.float32),
        "gate_vec": normal_values(key_list[7], (N_SECTION, 2, D), D ** -0.5, 0.21875, ((0, 4),), jnp.float32),
    }


HIGHEST_PRECISION = lax.Precision.HIGHEST
SCORE_SCALE = 0.125
MASK_FILL = -1e+30

@jax.custom_vjp
def low(v):
    return lax.optimization_barrier(v.astype(jnp.bfloat16)).astype(jnp.float32)

@jax.custom_vjp
def low_back(v):
    return v

def low_keep(v):
    return (low(v), None)

def low_pass(kept, grad):
    return (grad,)

def back_keep(v):
    return (v, None)

def back_low(kept, grad):
    return (low(grad),)
low.defvjp(low_keep, low_pass)
low_back.defvjp(back_keep, back_low)

def page_allowed(page_counts, cross_section):
    slot_index = jnp.arange(VIS + TXT, dtype=jnp.int32)
    visual_slot = slot_index < VIS
    live_slot = jnp.where(visual_slot[None, :], slot_index[None, :] < page_counts[:, 0:1], slot_index[None, :] - VIS < page_counts[:, 1:2])
    allowed = live_slot[:, None, None, :]
    if cross_section:
        allowed = jnp.logical_and(allowed, (visual_slot[:, None] != visual_slot[None, :])[None, None])
    return allowed

def gate_table(gate_pair):
    return jnp.concatenate([jnp.broadcast_to(gate_pair[1], (VIS, D)), jnp.broadcast_to(gate_pair[0], (TXT, D))], axis=0)

def attention_branch(section_in, weight_a, weight_b, allowed):
    page_total = section_in.shape[0]
    blocks = weight_b.reshape(4, D, D)
    proj_vis = jnp.einsum('pld,kde->plke', section_in[:, :VIS], blocks[:3], precision=HIGHEST_PRECISION).reshape(page_total, VIS, 3 * D)
    proj_txt = jnp.einsum('pld,de->ple', section_in[:, VIS:], weight_a[:, :3 * D], precision=HIGHEST_PRECISION)
    packed = low(low_back(jnp.concatenate([proj_vis, proj_txt], axis=1)))
    query_heads = packed[..., :D].reshape(page_total, VIS + TXT, HEADS, HEAD_DIM)
    key_heads = packed[..., D:2 * D].reshape(page_total, VIS + TXT, HEADS, HEAD_DIM)
    value_heads = packed[..., 2 * D:].reshape(page_total, VIS + TXT, HEADS, HEAD_DIM)
    scores = low_back(jnp.einsum('pqhe,pkhe->phqk', query_heads, key_heads, precision=HIGHEST_PRECISION) * SCORE_SCALE)
    scores = jnp.where(allowed, scores, MASK_FILL)
    attn_probs = low(jax.nn.softmax(scores, axis=-1))
    context = jnp.einsum('phqk,pkhe->pqhe', attn_probs, value_heads, precision=HIGHEST_PRECISION)
    context = low(low_back(context.reshape(page_total, VIS + TXT, D)))
    out_vis = jnp.einsum('pld,de->ple', context[:, :VIS], blocks[3], precision=HIGHEST_PRECISION)
    out_txt = jnp.einsum('pld,de->ple', context[:, VIS:], weight_a[:, 3 * D:], precision=HIGHEST_PRECISION)
    return low_back(jnp.concatenate([out_vis, out_txt], axis=1))

def feed_branch(section_in, weight_a, weight_b):
    hidden = low_back(jnp.einsum('pld,df->plf', section_in, weight_a, precision=HIGHEST_PRECISION))
    active = low(jax.nn.gelu(hidden))
    return low_back(jnp.einsum('plf,fd->pld', active, weight_b, precision=HIGHEST_PRECISION))

def section_tail(section_in, branch, gain_row, bias_row, gate_pair):
    gate_value = jax.nn.sigmoid(lax.optimization_barrier(jnp.sum(section_in * gate_table(gate_pair)[None], axis=-1)))
    mixed_sum = section_in + gate_value[..., None] * branch
    centred = mixed_sum - lax.optimization_barrier(jnp.mean(mixed_sum, axis=-1, keepdims=True))
    normed = centred * lax.rsqrt(lax.optimization_barrier(jnp.mean(centred * centred, axis=-1, keepdims=True)) + 1e-05)
    return normed * gain_row + bias_row

def run_section(section_in, page_counts, weight_a, weight_b, gain_row, bias_row, gate_pair, section_number):
    page_total = page_counts.shape[0]
    group_size = math.gcd(page_total, 32)

    def one_group(pieces):
        group_in, group_counts = pieces
        if section_number % 2 == 0:
            branch = attention_branch(group_in, weight_a, weight_b, page_allowed(group_counts, section_number == 0))
        else:
            branch = feed_branch(group_in, weight_a, weight_b)
        return section_tail(group_in, branch, gain_row, bias_row, gate_pair)
    shaped_in = section_in.reshape(page_total // group_size, group_size, VIS + TXT, D)
    shaped_counts = page_counts.reshape(page_total // group_size, group_size, 2)
    result = lax.map(jax.checkpoint(one_group), (shaped_in, shaped_counts))
    return result.reshape(page_total, VIS + TXT, D)

def reference(acts, cotan, counts, weight_in, weight_out, ln_gain, ln_bias, gate_vec):
    shape_pages = (PAGES, VIS + TXT, D)
    start_acts = acts.astype(jnp.float32).reshape(shape_pages)
    target = cotan.astype(jnp.float32).reshape(shape_pages)
    probes = jnp.zeros((N_SECTION - 1,) + shape_pages, jnp.float32)

    def forward(start_in, weight_a, weight_b, gains, biases, gates, probe_all):
        current = low_back(start_in)
        results = []
        for section_number in range(N_SECTION):
            result = low(run_section(current, counts, weight_a[section_number], weight_b[section_number], gains[section_number], biases[section_number], gates[section_number], section_number))
            results.append(result)
            if section_number + 1 < N_SECTION:
                current = low_back(result + probe_all[section_number])
        return (jnp.sum(target * results[-1]), jnp.stack(results))
    total_loss, back_fn, stacked = jax.vjp(forward, start_acts, weight_in.astype(jnp.float32), weight_out.astype(jnp.float32), ln_gain, ln_bias, gate_vec, probes, has_aux=True)
    gradients = back_fn(jnp.ones_like(total_loss))
    d_start, d_in, d_out, d_gain, d_bias, d_gate, d_probe = gradients
    input_grads = jnp.concatenate([d_start[None], d_probe], axis=0).reshape(N_SECTION, TOKENS, D).astype(jnp.bfloat16)
    section_outputs = stacked.reshape(N_SECTION, TOKENS, D).astype(jnp.bfloat16)
    return (section_outputs, input_grads, d_in, d_out, d_gain, d_bias, d_gate)
```

```python
import functools

import jax
import jax.numpy as jnp
from jax import lax
from jax.experimental import pallas as pl
from jax.experimental.pallas import tpu as pltpu
from jax.sharding import PartitionSpec as P

HEAD_DIM = 64
VIS = 16
TXT = 112
PAGE = VIS + TXT
SCORE_SCALE = 0.125
MASK_FILL = -1e30
GROUP = 1
CHUNKS = 12
LAG = 2
AHEAD = 2
GELU_A = 0.7978845608028654
GELU_B = 0.044715
F32 = jnp.float32
BF16 = jnp.bfloat16

VMEM = pl.BlockSpec(memory_space=pltpu.VMEM)
SMEM = pl.BlockSpec(memory_space=pltpu.SMEM)
HBM = pl.BlockSpec(memory_space=pltpu.HBM)


def dot(a, b):
    return jnp.dot(a, b, preferred_element_type=F32)


def dot_nt(a, b):
    return lax.dot_general(a, b, (((1,), (1,)), ((), ())), preferred_element_type=F32)


def dot_tn(a, b):
    return lax.dot_general(a, b, (((0,), (0,)), ((), ())), preferred_element_type=F32)


def text_of(value):
    pages = [value[i + VIS : i + PAGE] for i in range(0, value.shape[0], PAGE)]
    return pages[0] if len(pages) == 1 else jnp.concatenate(pages, axis=0)


def visual_of(value):
    pages = [value[i : i + VIS] for i in range(0, value.shape[0], PAGE)]
    return pages[0] if len(pages) == 1 else jnp.concatenate(pages, axis=0)


def to_pages(visual, text):
    pieces = []
    for i in range(visual.shape[0] // VIS):
        pieces += [visual[i * VIS : (i + 1) * VIS], text[i * TXT : (i + 1) * TXT]]
    return jnp.concatenate(pieces, axis=0)


def gate_table(vecs, rows, width):
    visual = lax.broadcasted_iota(jnp.int32, (rows, width), 0) % PAGE < VIS
    return jnp.where(visual, vecs[3:4, :], vecs[2:3, :])


def tail_parts(x, branch, gate_rows):
    gate = jax.nn.sigmoid(jnp.sum(x * gate_rows, axis=-1, keepdims=True))
    mixed = x + gate * branch
    centred = mixed - jnp.mean(mixed, axis=-1, keepdims=True)
    inv = lax.rsqrt(jnp.mean(centred * centred, axis=-1, keepdims=True) + 1e-05)
    return gate, centred * inv, inv


def allowed_pairs(counts, page, cross):
    query = lax.broadcasted_iota(jnp.int32, (2 * PAGE, PAGE), 0) % PAGE
    key = lax.broadcasted_iota(jnp.int32, (2 * PAGE, PAGE), 1)
    limit = jnp.where(key < VIS, counts[page, 0], counts[page, 1] + VIS)
    unlike = jnp.where(query < VIS, 1, 0) + jnp.where(key < VIS, 1, 0) - 1
    return key + (PAGE * cross) * (unlike * unlike) < limit


def stack_heads(pair):
    low = lax.broadcasted_iota(jnp.int32, pair.shape, 1) < HEAD_DIM
    zero = jnp.zeros_like(pair)
    return jnp.concatenate([jnp.where(low, pair, zero), jnp.where(low, zero, pair)], axis=0)


def side_by_side(stacked):
    return jnp.concatenate([stacked[:PAGE], stacked[PAGE:]], axis=1)


def pair_probs(query_rows, key_pair, allowed):
    scores = jnp.where(allowed, dot_nt(query_rows, key_pair) * SCORE_SCALE, MASK_FILL)
    top = jnp.max(scores, axis=-1, keepdims=True)
    weights = jnp.exp(scores - top)
    return weights / jnp.sum(weights, axis=-1, keepdims=True)


def load_kernel(*refs):
    count = len(refs) // 2
    sems = refs[-1]
    copies = [
        pltpu.make_async_copy(refs[i], refs[count + i], sems.at[i]) for i in range(count)
    ]
    for copy in copies:
        copy.start()
    for copy in copies:
        copy.wait()


def page_rows(first_page, i):
    return pl.ds(pl.multiple_of((first_page + i) * PAGE, PAGE), PAGE)


def slot_of(meta, tick, steps_in, pages, micro):
    index = tick - steps_in
    valid = jnp.logical_and(index >= 0, index * micro < pages * PAGE)
    kind = jnp.where(valid, 1 + meta[0] % 2, 0)
    last = pages - micro // PAGE
    return kind, jnp.clip(index * (micro // PAGE), 0, last)


def forward_kernel(
    meta, counts, incoming, w_in, w_out, vecs, *refs, state_in, tick
):
    y_ref, xin, out, sav, dh, br = refs[state_in:]
    micro, width = y_ref.shape
    group = micro // PAGE
    section = meta[0]
    kind, page = slot_of(meta, tick, section, counts.shape[0], micro)
    cross = jnp.where(section == 0, 1, 0)
    rows = pl.ds(pl.multiple_of(page * PAGE, PAGE), micro)

    def begin():
        x_low = jnp.where(section == 0, xin[rows, :], incoming[...])
        xin[rows, :] = x_low
        return x_low

    def finish(x_low, branch):
        br[rows, :] = branch
        gate, normed, inv = tail_parts(
            x_low.astype(F32), branch, gate_table(vecs, micro, width)
        )
        y = (normed * vecs[0:1, :] + vecs[1:2, :]).astype(BF16)
        y_ref[...] = y
        out[rows, :] = y

    @pl.when(kind == 1)
    def attention():
        x_low = begin()
        x_text, x_visual = text_of(x_low), visual_of(x_low)
        for k in range(3):
            cols = slice(k * width, (k + 1) * width)
            sav[rows, cols] = to_pages(
                dot(x_visual, w_out[cols, :]).astype(BF16), dot(x_text, w_in[:, cols]).astype(BF16)
            )
        for i in range(group):
            here = page_rows(page, i)
            allowed = allowed_pairs(counts, page + i, cross)
            for lane in range(0, width, 2 * HEAD_DIM):
                query_rows = stack_heads(sav[here, lane : lane + 128])
                probs = pair_probs(query_rows, sav[here, width + lane : width + lane + 128], allowed)
                values = stack_heads(sav[here, 2 * width + lane : 2 * width + lane + 128])
                sav[here, 3 * width + lane : 3 * width + lane + 128] = dot(
                    side_by_side(probs.astype(BF16)), values
                ).astype(BF16)
        context = sav[rows, 3 * width :]
        finish(
            x_low,
            to_pages(
                dot(visual_of(context), w_out[3 * width :, :]),
                dot(text_of(context), w_in[:, 3 * width :]),
            ),
        )

    @pl.when(kind == 2)
    def feed():
        x_low = begin()
        branch = None
        for j in range(w_in.shape[1] // width):
            cols = slice(j * width, (j + 1) * width)
            hidden = dot(x_low, w_in[:, cols])
            square = hidden * hidden
            tanh = jnp.tanh(hidden * (GELU_A + (GELU_A * GELU_B) * square))
            half = 0.5 + 0.5 * tanh
            active = (hidden * half).astype(BF16)
            sav[rows, cols] = active
            slope = half + (hidden * (half * (1.0 - tanh))) * (
                GELU_A + (3.0 * GELU_A * GELU_B) * square
            )
            dh[rows, cols] = slope.astype(BF16)
            part = dot(active, w_out[cols, :])
            branch = part if branch is None else branch + part
        finish(x_low, branch)


def backward_kernel(
    meta, counts, incoming, w_in, w_out, vecs, *refs, state_in, tick, sections
):
    dx_ref, xin, out, sav, dh, br, grads, db, small, dc = refs[state_in:]
    micro, width = dx_ref.shape
    group = micro // PAGE
    section = meta[0]
    last = sections - 1
    kind, page = slot_of(meta, tick, last - section, counts.shape[0], micro)
    cross = jnp.where(section == 0, 1, 0)
    rows = pl.ds(pl.multiple_of(page * PAGE, PAGE), micro)

    def tail():
        x = xin[rows, :].astype(F32)
        branch = br[rows, :]
        gate_rows = gate_table(vecs, micro, width)
        gate, normed, inv = tail_parts(x, branch, gate_rows)
        dy = jnp.where(section == last, grads[rows, :], incoming[...]).astype(F32)
        dn = dy * vecs[0:1, :]
        du = inv * (
            dn
            - jnp.mean(dn, axis=-1, keepdims=True)
            - normed * jnp.mean(dn * normed, axis=-1, keepdims=True)
        )
        dbranch = (du * gate).astype(BF16)
        db[rows, :] = dbranch
        dz = jnp.sum(du * branch, axis=-1, keepdims=True) * gate * (1.0 - gate)
        weighted = dz * x
        small[pl.ds(pl.multiple_of(page * 8, 8), 8), :] = jnp.concatenate(
            [
                jnp.sum(dy * normed, axis=0, keepdims=True),
                jnp.sum(dy, axis=0, keepdims=True),
                jnp.sum(text_of(weighted), axis=0, keepdims=True),
                jnp.sum(visual_of(weighted), axis=0, keepdims=True),
                jnp.zeros((4, width), F32),
            ],
            axis=0,
        )
        return dbranch, du + dz * gate_rows

    def finish(total):
        dx = total.astype(BF16)
        dx_ref[...] = dx
        grads[rows, :] = dx

    @pl.when(kind == 1)
    def attention():
        dbranch, dres = tail()
        dc[...] = to_pages(
            dot_nt(visual_of(dbranch), w_out[3 * width :, :]).astype(BF16),
            dot_nt(text_of(dbranch), w_in[:, 3 * width :]).astype(BF16),
        )
        for i in range(group):
            here = page_rows(page, i)
            own = slice(i * PAGE, (i + 1) * PAGE)
            allowed = allowed_pairs(counts, page + i, cross)
            for lane in range(0, width, 2 * HEAD_DIM):
                key_pair = sav[here, width + lane : width + lane + 128]
                query_rows = stack_heads(sav[here, lane : lane + 128])
                probs = pair_probs(query_rows, key_pair, allowed)
                context_rows = stack_heads(dc[own, lane : lane + 128])
                dprobs = dot_nt(
                    context_rows, sav[here, 2 * width + lane : 2 * width + lane + 128]
                )
                dscores = (
                    probs * (dprobs - jnp.sum(dprobs * probs, axis=-1, keepdims=True))
                ).astype(BF16)
                dh[here, 2 * width + lane : 2 * width + lane + 128] = dot_tn(
                    probs.astype(BF16), context_rows
                ).astype(BF16)
                dh[here, width + lane : width + lane + 128] = (
                    dot_tn(dscores, query_rows) * SCORE_SCALE
                ).astype(BF16)
                dh[here, lane : lane + 128] = (
                    dot(side_by_side(dscores), stack_heads(key_pair)) * SCORE_SCALE
                ).astype(BF16)
        text, visual = None, None
        for k in range(3):
            cols = slice(k * width, (k + 1) * width)
            part = dh[rows, cols]
            one = dot_nt(text_of(part), w_in[:, cols])
            two = dot_nt(visual_of(part), w_out[cols, :])
            text = one if text is None else text + one
            visual = two if visual is None else visual + two
        finish(dres + to_pages(visual, text))

    @pl.when(kind == 2)
    def feed():
        dbranch, total = tail()
        for j in range(w_in.shape[1] // width):
            cols = slice(j * width, (j + 1) * width)
            dhidden = (dot_nt(dbranch, w_out[cols, :]) * dh[rows, cols].astype(F32)).astype(BF16)
            dh[rows, cols] = dhidden
            total = total + dot_nt(dhidden, w_in[:, cols])
        finish(total)


def weight_chunk(kind, core, xin, sav, dh, db, own_ref, other_ref, chunk):
    part, width = own_ref.shape
    start = chunk * part
    cols = slice(start, start + part)

    def put(grad_a, grad_b):
        low_a = jnp.concatenate(
            [grad_a[i : i + part].astype(BF16) for i in range(0, width, part)], axis=1
        )
        low_b = grad_b.astype(BF16)
        own_ref[...] = jnp.where(core == 0, low_a, low_b)
        other_ref[...] = jnp.where(core == 0, low_b, low_a)

    @pl.when(kind == 1)
    def attention():
        block, inner = start // width, start % width
        inner_cols = slice(inner, inner + part)
        if block < 3:
            left, right = xin[...], dh[:, block * width : (block + 1) * width]
            put(
                dot_tn(text_of(left), text_of(dh[:, cols])),
                dot_tn(visual_of(left[:, inner_cols]), visual_of(right)),
            )
        else:
            left, right = sav[:, 3 * width :], db[...]
            put(
                dot_tn(text_of(left), text_of(right[:, inner_cols])),
                dot_tn(visual_of(left[:, inner_cols]), visual_of(right)),
            )

    @pl.when(kind == 2)
    def feed():
        put(dot_tn(xin[...], dh[:, cols]), dot_tn(sav[:, cols], db[...]))


def work_kernel(*refs, chunk, place, placed):
    refs = list(refs)
    meta, _ = refs.pop(0), refs.pop(0)
    core = meta[1] % 2
    if chunk is not None:
        factors, refs = refs[:4], refs[4:]
    if place is not None:
        (own, other), refs = refs[:2], refs[2 + placed :]
    if chunk is not None:
        (own_ref, other_ref), refs = refs[:2], refs[2:]
    if place is not None:
        (grad_in, grad_out), refs = refs[:2], refs[2:]
    token = refs.pop(0)
    token[...] = jnp.zeros_like(token)
    copies = []
    if place is not None:
        buf_a, buf_b, sems = refs
        part, width = buf_b.shape
        start = place * part
        mine, theirs = own[...], other[...]
        buf_b[...] = jnp.where(core == 0, theirs, mine).astype(F32)
        copies.append(
            pltpu.make_async_copy(buf_b, grad_out.at[pl.ds(start, part), :], sems.at[0])
        )
        copies[0].start()
        for i in range(width // part):
            cols = slice(i * part, (i + 1) * part)
            buf_a[cols, :] = jnp.where(core == 0, mine[:, cols], theirs[:, cols]).astype(F32)
        copies.append(
            pltpu.make_async_copy(buf_a, grad_in.at[:, pl.ds(start, part)], sems.at[1])
        )
        copies[1].start()
    if chunk is not None:
        weight_chunk(1 + meta[0] % 2, core, *factors, own_ref, other_ref, chunk)
    for copy in copies:
        copy.wait()


def relay_kernel(*refs, new, inner, total, final):
    refs = list(refs)
    meta, _ = refs.pop(0), refs.pop(0)
    chip = meta[1] // 2

    def take(count):
        taken = [ref[...] for ref in refs[:count]]
        del refs[:count]
        return taken

    def add(a, b):
        return (a.astype(F32) + b.astype(F32)).astype(BF16)

    new_in = take(2) if new else None
    inner_in = take(1) if inner else None
    total_in = take(1) if total else None
    final_in = take(1) if final else None
    got_right, got_left = take(2) if (inner or total or final) else (None, None)
    left_half = chip < 2
    middle = jnp.logical_or(chip == 1, chip == 2)
    sends = []
    if new:
        value = add(*new_in)
        refs.pop(0)[...] = value
        sends.append((value, 0))
    if inner:
        value = add(inner_in[0], jnp.where(left_half, got_right, got_left))
        refs.pop(0)[...] = value
        sends.append((value, 1))
    if total:
        value = add(total_in[0], jnp.where(left_half, got_left, got_right))
        refs.pop(0)[...] = value
        sends.append((value, 2))
    if final:
        refs.pop(0)[...] = jnp.where(
            middle, final_in[0], jnp.where(left_half, got_left, got_right)
        )
    if sends:
        right, left = sends[0][0], sends[0][0]
        for value, place in sends[1:]:
            right = jnp.where(chip == place, value, right)
            left = jnp.where(chip == 3 - place, value, left)
        refs.pop(0)[...] = right
        refs.pop(0)[...] = left
    token = refs.pop(0)
    token[...] = jnp.zeros_like(token)


def sum_pages_kernel(small, total_ref, *, group):
    total = small[0:8, :]
    for i in range(8 * group, small.shape[0], 8 * group):
        total += small[i : i + 8, :]
    total_ref[...] = total


def add_kernel(a, b, total):
    total[...] = a[...] + b[...]


def struct(shape, dtype):
    return jax.ShapeDtypeStruct(shape, dtype)


def params(mebibytes):
    return pltpu.CompilerParams(vmem_limit_bytes=mebibytes << 20)


def in_vmem(*arrays):
    return [pltpu.with_memory_space_constraint(a, pltpu.VMEM) for a in arrays]


def run_load(*arrays):
    return pl.pallas_call(
        load_kernel,
        out_shape=[pltpu.VMEM(a.shape, a.dtype) for a in arrays],
        in_specs=[HBM] * len(arrays),
        out_specs=[VMEM] * len(arrays),
        scratch_shapes=[pltpu.SemaphoreType.DMA((len(arrays),))],
        compiler_params=params(4),
        name="load_weights",
    )(*[pltpu.with_memory_space_constraint(a, pltpu.HBM) for a in arrays])


def run_forward(tick, meta, counts, incoming, w_in, w_out, vecs, state):
    rows, width = state[0].shape
    hidden = w_in.shape[1]
    return pl.pallas_call(
        functools.partial(forward_kernel, state_in=len(state), tick=tick),
        out_shape=[
            struct(incoming.shape, BF16),
            pltpu.VMEM((rows, width), BF16),
            pltpu.VMEM((rows, width), BF16),
            pltpu.VMEM((rows, hidden), BF16),
            pltpu.VMEM((rows, hidden), BF16),
            pltpu.VMEM((rows, width), F32),
        ],
        in_specs=[SMEM, SMEM] + [VMEM] * (4 + len(state)),
        out_specs=[VMEM] * 6,
        input_output_aliases={6 + i: 1 + i for i in range(len(state))},
        compiler_params=params(12),
        name="forward_page",
    )(meta, counts, incoming, *in_vmem(w_in, w_out), vecs, *state)


def run_backward(tick, sections, meta, counts, incoming, w_in, w_out, vecs, state, back):
    rows, width = back[0].shape
    every = list(state) + list(back)
    return pl.pallas_call(
        functools.partial(
            backward_kernel, state_in=len(every), tick=tick, sections=sections
        ),
        out_shape=[struct(incoming.shape, BF16)]
        + [pltpu.VMEM(s.shape, s.dtype) for s in state]
        + [
            pltpu.VMEM((rows, width), BF16),
            pltpu.VMEM((rows, width), BF16),
            pltpu.VMEM((8 * rows // PAGE, width), F32),
        ],
        in_specs=[SMEM, SMEM] + [VMEM] * (4 + len(every)),
        out_specs=[VMEM] * 9,
        input_output_aliases={6 + i: 1 + i for i in range(len(every))},
        scratch_shapes=[pltpu.VMEM(incoming.shape, BF16)],
        compiler_params=params(12),
        name="backward_page",
    )(meta, counts, incoming, *in_vmem(w_in, w_out), vecs, *every)


TOKEN = (8, 128)


def run_work(meta, token, factors, chunk, totals, place, grads):
    width = factors[0].shape[1]
    hidden = factors[1].shape[1]
    part = hidden // CHUNKS
    inputs, specs = [meta, token], [SMEM, VMEM]
    outs, out_specs, scratch, aliases = [], [], [], {}
    if chunk is not None:
        inputs += in_vmem(*factors)
        specs += [VMEM] * 4
        outs += [struct((part, width), BF16)] * 2
        out_specs += [VMEM] * 2
    if place is not None:
        inputs += list(totals)
        specs += [VMEM] * 2
        aliases = {len(inputs) + i: len(outs) + i for i in range(len(grads))}
        inputs += list(grads)
        specs += [HBM] * len(grads)
        outs += [pltpu.HBM((width, hidden), F32), pltpu.HBM((hidden, width), F32)]
        out_specs += [HBM] * 2
        scratch = [
            pltpu.VMEM((width, part), F32),
            pltpu.VMEM((part, width), F32),
            pltpu.SemaphoreType.DMA((2,)),
        ]
    got = pl.pallas_call(
        functools.partial(work_kernel, chunk=chunk, place=place, placed=len(grads)),
        out_shape=outs + [struct(TOKEN, F32)],
        in_specs=specs,
        out_specs=out_specs + [VMEM],
        input_output_aliases=aliases,
        scratch_shapes=scratch,
        compiler_params=params(16),
        name="weight_chunk",
    )(*inputs)
    *got, token = got
    made = got[:2] if chunk is not None else None
    return made, (got[-2:] if place is not None else grads), token


def run_relay(meta, token, new, inner, total, final, got):
    inputs = [*(new or ()), *(inner or ()), *(total or ()), *(final or ()), *(got or ())]
    sends = bool(new or inner or total)
    count = sum(bool(x) for x in (new, inner, total, final)) + 2 * sends
    shape = struct(inputs[0].shape, BF16)
    out = pl.pallas_call(
        functools.partial(
            relay_kernel, new=bool(new), inner=bool(inner), total=bool(total), final=bool(final)
        ),
        out_shape=[shape] * count + [struct(TOKEN, F32)],
        in_specs=[SMEM] + [VMEM] * (1 + len(inputs)),
        out_specs=[VMEM] * (count + 1),
        compiler_params=params(8),
        name="relay_chunk",
    )(meta, token, *inputs)
    *out, token = out
    kept = [out.pop(0) if x else None for x in (new, inner, total, final)]
    return kept, (out if sends else None), token


def sum_over_line(meta, token, factors, count):
    swap = [(i, i ^ 1) for i in range(8)]
    right = [(i, i + 2) for i in range(6)]
    left = [(i + 2, i) for i in range(6)]
    lag = LAG
    made, firsts, inners, totals, finals, got = {}, {}, {}, {}, {}, {}
    grads = ()

    def work(token, chunk, place):
        chunk = chunk if chunk is not None and chunk < count else None
        place = place if place is not None and 0 <= place < count else None
        if chunk is None and place is None:
            return token, grads
        pair = finals.pop(place) if place is not None else None
        new, grads_now, token = run_work(meta, token, factors, chunk, pair, place, grads)
        if new:
            made[chunk] = (new[0], lax.ppermute(new[1], "dp", swap))
        return token, grads_now

    for k in range(AHEAD):
        token, grads = work(token, k, None)
    for tick in range(count + 3 * lag):
        def at(stage):
            k = tick - stage * lag
            return k if 0 <= k < count else None

        new, inner, total, final = (at(i) for i in range(4))
        kept, sends, token = run_relay(
            meta,
            token,
            made.pop(new) if new is not None else None,
            (firsts.pop(inner),) if inner is not None else None,
            (inners.pop(total),) if total is not None else None,
            (totals.pop(final),) if final is not None else None,
            got.pop(tick) if tick in got else None,
        )
        if new is not None:
            firsts[new] = kept[0]
        if inner is not None:
            inners[inner] = kept[1]
        if total is not None:
            totals[total] = kept[2]
        if sends:
            got[tick + lag] = (
                lax.ppermute(sends[0], "dp", right),
                lax.ppermute(sends[1], "dp", left),
            )
        if final is not None:
            finals[final] = (kept[3], lax.ppermute(kept[3], "dp", swap))
        token, grads = work(token, tick + AHEAD, tick - 3 * lag - 1)
    token, grads = work(token, None, count - 1)
    return grads


def sum_small(small):
    rows, width = small.shape
    def call(kernel, *arrays):
        return pl.pallas_call(
            kernel,
            out_shape=struct((8, width), F32),
            in_specs=[VMEM] * len(arrays),
            out_specs=VMEM,
            compiler_params=params(4),
            name="small_sum",
        )(*arrays)

    total = call(functools.partial(sum_pages_kernel, group=GROUP), *in_vmem(small))
    size = lax.axis_size("dp")
    if size & (size - 1):
        return lax.psum(total, "dp")
    step = 1
    while step < size:
        total = call(
            add_kernel, total, lax.ppermute(total, "dp", [(i, i ^ step) for i in range(size)])
        )
        step *= 2
    return total


def body(acts, cotan, counts, weight_in, weight_out, ln_gain, ln_bias, gate_vec):
    section = lax.axis_index("section")
    sections = lax.axis_size("section")
    dp_index = lax.axis_index("dp")
    dp_size = lax.axis_size("dp")
    rows, width = acts.shape
    micros = rows // (GROUP * PAGE)
    vecs = jnp.concatenate(
        [ln_gain, ln_bias, gate_vec[0], jnp.zeros((4, width), F32)], axis=0
    )
    meta = jnp.stack([section, dp_index]).astype(jnp.int32)
    incoming = jnp.zeros((GROUP * PAGE, width), BF16)
    vecs, meta, counts, incoming, w_in, w_out, acts, cotan = lax.optimization_barrier(
        (vecs, meta, counts, incoming, weight_in[0], weight_out[0], acts, cotan)
    )
    w_in, w_out, acts, cotan = run_load(w_in, w_out, acts, cotan)
    core = dp_index % 2
    upstream = incoming
    state, back = (acts,), (cotan,)
    for tick in range(micros + 2 * (sections - 1)):
        if tick < micros + sections - 1:
            y, *state = run_forward(
                tick, meta, counts, incoming, w_in, w_out, vecs, state
            )
            pairs = [(a, a + 1) for a in range(sections - 1) if 0 <= tick - a < micros]
            if pairs:
                incoming = lax.ppermute(y, "section", pairs)
        slot = tick - (sections - 1)
        if slot >= 0:
            dx, *both = run_backward(
                slot, sections, meta, counts, upstream, w_in, w_out, vecs, state, back
            )
            state, back = both[:5], both[5:]
            pairs = [
                (a, a - 1)
                for a in range(1, sections)
                if 0 <= slot - (sections - 1 - a) < micros
            ]
            if pairs:
                upstream = lax.ppermute(dx, "section", pairs)
    xin, outputs, sav, dh, branch = state
    grads, db, small = back
    small_sum = sum_small(small)
    factors = (xin, sav, dh, db)
    if dp_size == 8:
        grad_in, grad_out = sum_over_line(meta, jnp.zeros(TOKEN, F32), factors, CHUNKS)
    else:
        so_far, token = (), jnp.zeros(TOKEN, F32)
        for k in range(CHUNKS):
            (own, other), so_far, token = run_work(meta, token, factors, k, None, None, so_far)
            pair = jnp.where(core == 0, jnp.stack([own, other]), jnp.stack([other, own]))
            pair = lax.psum(pair, "dp")
            pair = jnp.where(core == 0, pair, pair[::-1])
            _, so_far, token = run_work(meta, token, factors, None, (pair[0], pair[1]), k, so_far)
        grad_in, grad_out = so_far
    return (
        outputs[None],
        grads[None],
        grad_in[None],
        grad_out[None],
        small_sum[0:1],
        small_sum[1:2],
        small_sum[2:4][None],
    )


def solution(mesh):
    return jax.shard_map(
        body,
        mesh=mesh,
        in_specs=(
            P("dp", None),
            P("dp", None),
            P("dp", None),
            P("section", None, None),
            P("section", None, None),
            P("section", None),
            P("section", None),
            P("section", None, None),
        ),
        out_specs=(
            P("section", "dp", None),
            P("section", "dp", None),
            P("section", None, None),
            P("section", None, None),
            P("section", None),
            P("section", None),
            P("section", None, None),
        ),
        check_vma=False,
    )
```

```python
import functools

import jax
import jax.numpy as jnp
from jax import lax
from jax.experimental import pallas as pl
from jax.experimental.pallas import tpu as pltpu
from jax.sharding import PartitionSpec as P

HEAD_DIM = 64
VIS = 16
TXT = 112
PAGE = VIS + TXT
SCORE_SCALE = 0.125
MASK_FILL = -1e30
GROUP = 2
CHUNKS = 12
LAG = 3
AHEAD = 2
BACK_LAG = 2
GELU_A = 0.7978845608028654
GELU_B = 0.044715
F32 = jnp.float32
BF16 = jnp.bfloat16

VMEM = pl.BlockSpec(memory_space=pltpu.VMEM)
SMEM = pl.BlockSpec(memory_space=pltpu.SMEM)
HBM = pl.BlockSpec(memory_space=pltpu.HBM)


def dot(a, b):
    return jnp.dot(a, b, preferred_element_type=F32)


def dot_nt(a, b):
    return lax.dot_general(a, b, (((1,), (1,)), ((), ())), preferred_element_type=F32)


def dot_tn(a, b):
    return lax.dot_general(a, b, (((0,), (0,)), ((), ())), preferred_element_type=F32)


def text_of(value):
    pages = [value[i + VIS : i + PAGE] for i in range(0, value.shape[0], PAGE)]
    return pages[0] if len(pages) == 1 else jnp.concatenate(pages, axis=0)


def visual_of(value):
    pages = [value[i : i + VIS] for i in range(0, value.shape[0], PAGE)]
    return pages[0] if len(pages) == 1 else jnp.concatenate(pages, axis=0)


def to_pages(visual, text):
    pieces = []
    for i in range(visual.shape[0] // VIS):
        pieces += [visual[i * VIS : (i + 1) * VIS], text[i * TXT : (i + 1) * TXT]]
    return jnp.concatenate(pieces, axis=0)


def gate_table(vecs, rows, width):
    visual = lax.broadcasted_iota(jnp.int32, (rows, width), 0) % PAGE < VIS
    return jnp.where(visual, vecs[3:4, :], vecs[2:3, :])


def tail_parts(x, branch, gate_rows):
    gate = jax.nn.sigmoid(jnp.sum(x * gate_rows, axis=-1, keepdims=True))
    mixed = x + gate * branch
    centred = mixed - jnp.mean(mixed, axis=-1, keepdims=True)
    inv = lax.rsqrt(jnp.mean(centred * centred, axis=-1, keepdims=True) + 1e-05)
    return gate, centred * inv, inv


def allowed_pairs(limit_row, cross):
    key = lax.broadcasted_iota(jnp.int32, (PAGE, 2 * PAGE), 0)
    query = lax.broadcasted_iota(jnp.int32, (PAGE, 2 * PAGE), 1) % PAGE
    limit = jnp.where(key < VIS, limit_row[:, : 2 * PAGE], limit_row[:, 2 * PAGE :])
    unlike = jnp.where(query < VIS, 1, 0) + jnp.where(key < VIS, 1, 0) - 1
    return key + (PAGE * cross) * (unlike * unlike) < limit


def low_lanes(shape):
    return lax.broadcasted_iota(jnp.int32, shape, 1) < HEAD_DIM


def stack_heads(pair):
    low = low_lanes(pair.shape)
    zero = jnp.zeros_like(pair)
    return jnp.concatenate([jnp.where(low, pair, zero), jnp.where(low, zero, pair)], axis=0)


def unstack_heads(stacked):
    half = stacked.shape[0] // 2
    top = stacked[:half]
    return jnp.where(low_lanes(top.shape), top, stacked[half:])


def pair_probs(key_pair, query_rows, allowed):
    scores = jnp.where(allowed, dot_nt(key_pair, query_rows) * SCORE_SCALE, MASK_FILL)
    top = jnp.max(scores, axis=0, keepdims=True)
    weights = jnp.exp(scores - top)
    return weights / jnp.sum(weights, axis=0, keepdims=True)


def load_kernel(*refs, count):
    sources, live_in = refs[: count + 3], refs[count + 3]
    vecs, limits = refs[count + 4 : count + 6]
    targets = refs[count + 6 : 2 * count + 6]
    gain, bias, gates, live, sems = refs[2 * count + 6 :]
    targets = (*targets, gain, bias, gates)
    copies = [
        pltpu.make_async_copy(source, target, sems.at[i])
        for i, (source, target) in enumerate(zip(sources, targets))
    ]
    live_copy = pltpu.make_async_copy(live_in, live, sems.at[count + 3])
    for copy in copies[count:] + [live_copy] + copies[:count]:
        copy.start()
    for copy in copies[count:] + [live_copy]:
        copy.wait()
    vecs[0:1, :] = gain[...]
    vecs[1:2, :] = bias[...]
    vecs[2:4, :] = gates[...]
    first = lax.broadcasted_iota(jnp.int32, (1, 4 * PAGE), 1) < 2 * PAGE
    for page in range(limits.shape[0]):
        limits[page : page + 1, :] = jnp.where(first, live[0, page], live[1, page] + VIS)
    for copy in copies[:count]:
        copy.wait()


def page_rows(first_page, i):
    return pl.ds(pl.multiple_of((first_page + i) * PAGE, PAGE), PAGE)


def slot_of(section, tick, steps_in, pages, micro):
    index = tick - steps_in
    valid = jnp.logical_and(index >= 0, index * micro < pages * PAGE)
    kind = jnp.where(valid, 1 + section % 2, 0)
    last = pages - micro // PAGE
    return kind, jnp.clip(index * (micro // PAGE), 0, last)


def forward_kernel(
    limits, incoming, w_in, w_out, vecs, *refs, state_in, tick
):
    y_ref, xin, out, sav, dh, br, probs_ref = refs[state_in:]
    micro, width = y_ref.shape
    group = micro // PAGE
    section = lax.axis_index("section")
    kind, page = slot_of(section, tick, section, limits.shape[0], micro)
    cross = jnp.where(section == 0, 1, 0)
    rows = pl.ds(pl.multiple_of(page * PAGE, PAGE), micro)

    def begin():
        x_low = jnp.where(section == 0, xin[rows, :], incoming[...])
        xin[rows, :] = x_low
        return x_low

    def finish(x_low, branch):
        br[rows, :] = branch
        gate, normed, inv = tail_parts(
            x_low.astype(F32), branch, gate_table(vecs, micro, width)
        )
        y = (normed * vecs[0:1, :] + vecs[1:2, :]).astype(BF16)
        y_ref[...] = y
        out[rows, :] = y

    @pl.when(kind == 1)
    def attention():
        x_low = begin()
        x_text, x_visual = text_of(x_low), visual_of(x_low)
        for k in range(3):
            cols = slice(k * width, (k + 1) * width)
            sav[rows, cols] = to_pages(
                dot(x_visual, w_out[cols, :]).astype(BF16), dot(x_text, w_in[:, cols]).astype(BF16)
            )
        for i in range(group):
            here = page_rows(page, i)
            allowed = allowed_pairs(limits[pl.ds(page + i, 1), :], cross)
            for lane in range(0, width, 2 * HEAD_DIM):
                query_rows = stack_heads(sav[here, lane : lane + 128])
                probs = pair_probs(
                    sav[here, width + lane : width + lane + 128], query_rows, allowed
                ).astype(BF16)
                probs_ref[here, 2 * lane : 2 * lane + 2 * PAGE] = probs
                values = sav[here, 2 * width + lane : 2 * width + lane + 128]
                sav[here, 3 * width + lane : 3 * width + lane + 128] = unstack_heads(
                    dot_tn(probs, values)
                ).astype(BF16)
        context = sav[rows, 3 * width :]
        finish(
            x_low,
            to_pages(
                dot(visual_of(context), w_out[3 * width :, :]),
                dot(text_of(context), w_in[:, 3 * width :]),
            ),
        )

    @pl.when(kind == 2)
    def feed():
        x_low = begin()
        branch = None
        for j in range(w_in.shape[1] // width):
            cols = slice(j * width, (j + 1) * width)
            hidden = dot(x_low, w_in[:, cols])
            square = hidden * hidden
            tanh = jnp.tanh(hidden * (GELU_A + (GELU_A * GELU_B) * square))
            half = 0.5 + 0.5 * tanh
            active = (hidden * half).astype(BF16)
            sav[rows, cols] = active
            slope = half + (hidden * (half * (1.0 - tanh))) * (
                GELU_A + (3.0 * GELU_A * GELU_B) * square
            )
            dh[rows, cols] = slope.astype(BF16)
            part = dot(active, w_out[cols, :])
            branch = part if branch is None else branch + part
        finish(x_low, branch)


def backward_kernel(
    incoming, w_in, w_out, vecs, *refs, state_in, tick, sections
):
    dx_ref, xin, out, sav, dh, br, probs_ref, grads, db, small, dc = refs[state_in:]
    micro, width = dx_ref.shape
    group = micro // PAGE
    section = lax.axis_index("section")
    last = sections - 1
    kind, page = slot_of(section, tick, BACK_LAG * (last - section), xin.shape[0] // PAGE, micro)
    rows = pl.ds(pl.multiple_of(page * PAGE, PAGE), micro)

    def tail():
        x = xin[rows, :].astype(F32)
        branch = br[rows, :]
        gate_rows = gate_table(vecs, micro, width)
        gate, normed, inv = tail_parts(x, branch, gate_rows)
        dy = jnp.where(section == last, grads[rows, :], incoming[...]).astype(F32)
        dn = dy * vecs[0:1, :]
        du = inv * (
            dn
            - jnp.mean(dn, axis=-1, keepdims=True)
            - normed * jnp.mean(dn * normed, axis=-1, keepdims=True)
        )
        dbranch = (du * gate).astype(BF16)
        db[rows, :] = dbranch
        dz = jnp.sum(du * branch, axis=-1, keepdims=True) * gate * (1.0 - gate)
        weighted = dz * x
        small[pl.ds(pl.multiple_of(page * 8, 8), 8), :] = jnp.concatenate(
            [
                jnp.sum(dy * normed, axis=0, keepdims=True),
                jnp.sum(dy, axis=0, keepdims=True),
                jnp.sum(text_of(weighted), axis=0, keepdims=True),
                jnp.sum(visual_of(weighted), axis=0, keepdims=True),
                jnp.zeros((4, width), F32),
            ],
            axis=0,
        )
        return dbranch, du + dz * gate_rows

    def finish(total):
        dx = total.astype(BF16)
        dx_ref[...] = dx
        grads[rows, :] = dx

    @pl.when(kind == 1)
    def attention():
        dbranch, dres = tail()
        dc[...] = to_pages(
            dot_nt(visual_of(dbranch), w_out[3 * width :, :]).astype(BF16),
            dot_nt(text_of(dbranch), w_in[:, 3 * width :]).astype(BF16),
        )
        for i in range(group):
            here = page_rows(page, i)
            own = slice(i * PAGE, (i + 1) * PAGE)
            for lane in range(0, width, 2 * HEAD_DIM):
                key_pair = sav[here, width + lane : width + lane + 128]
                query_rows = stack_heads(sav[here, lane : lane + 128])
                probs_low = probs_ref[here, 2 * lane : 2 * lane + 2 * PAGE]
                probs = probs_low.astype(F32)
                context_rows = stack_heads(dc[own, lane : lane + 128])
                dprobs = dot_nt(
                    sav[here, 2 * width + lane : 2 * width + lane + 128], context_rows
                )
                dscores = (
                    probs * (dprobs - jnp.sum(dprobs * probs, axis=0, keepdims=True))
                ).astype(BF16)
                dh[here, 2 * width + lane : 2 * width + lane + 128] = dot(
                    probs_low, context_rows
                ).astype(BF16)
                dh[here, width + lane : width + lane + 128] = (
                    dot(dscores, query_rows) * SCORE_SCALE
                ).astype(BF16)
                dh[here, lane : lane + 128] = (
                    unstack_heads(dot_tn(dscores, key_pair)) * SCORE_SCALE
                ).astype(BF16)
        text, visual = None, None
        for k in range(3):
            cols = slice(k * width, (k + 1) * width)
            part = dh[rows, cols]
            one = dot_nt(text_of(part), w_in[:, cols])
            two = dot_nt(visual_of(part), w_out[cols, :])
            text = one if text is None else text + one
            visual = two if visual is None else visual + two
        finish(dres + to_pages(visual, text))

    @pl.when(kind == 2)
    def feed():
        dbranch, total = tail()
        for j in range(w_in.shape[1] // width):
            cols = slice(j * width, (j + 1) * width)
            dhidden = (dot_nt(dbranch, w_out[cols, :]) * dh[rows, cols].astype(F32)).astype(BF16)
            dh[rows, cols] = dhidden
            total = total + dot_nt(dhidden, w_in[:, cols])
        finish(total)


def weight_chunk(kind, core, xin, sav, dh, db, own_ref, other_ref, chunk):
    part, width = own_ref.shape
    start = chunk * part
    cols = slice(start, start + part)

    def put(grad_a, grad_b):
        low_a = jnp.concatenate(
            [grad_a[i : i + part].astype(BF16) for i in range(0, width, part)], axis=1
        )
        low_b = grad_b.astype(BF16)
        own_ref[...] = jnp.where(core == 0, low_a, low_b)
        other_ref[...] = jnp.where(core == 0, low_b, low_a)

    @pl.when(kind == 1)
    def attention():
        block, inner = start // width, start % width
        inner_cols = slice(inner, inner + part)
        if block < 3:
            left, right = xin[...], dh[:, block * width : (block + 1) * width]
            put(
                dot_tn(text_of(left), text_of(dh[:, cols])),
                dot_tn(visual_of(left[:, inner_cols]), visual_of(right)),
            )
        else:
            left, right = sav[:, 3 * width :], db[...]
            put(
                dot_tn(text_of(left), text_of(right[:, inner_cols])),
                dot_tn(visual_of(left[:, inner_cols]), visual_of(right)),
            )

    @pl.when(kind == 2)
    def feed():
        put(dot_tn(xin[...], dh[:, cols]), dot_tn(sav[:, cols], db[...]))


def work_kernel(*refs, chunk, place, placed, flush):
    refs = list(refs)
    del refs[0]
    core = lax.axis_index("dp") % 2

    def take(count):
        taken = refs[:count]
        del refs[:count]
        return taken

    factors = take(4) if chunk is not None else None
    rows_in = take(flush)
    if place is not None:
        own, other = take(2)
        take(placed)
    partial = take(2) if chunk is not None else None
    rows_out = take(flush)
    if place is not None:
        grad_in, grad_out = take(2)
    (token,) = take(1)
    token[...] = jnp.zeros_like(token)
    copies = []
    if flush:
        row_sems = refs.pop()
        for i, (source, target) in enumerate(zip(rows_in, rows_out)):
            copies.append(pltpu.make_async_copy(source, target, row_sems.at[i]))
            copies[-1].start()
    if place is not None:
        buf_a, buf_b, sems = refs
        part, width = buf_b.shape
        start = place * part
        mine, theirs = own[...], other[...]
        buf_b[...] = jnp.where(core == 0, theirs, mine).astype(F32)
        copies.append(
            pltpu.make_async_copy(buf_b, grad_out.at[pl.ds(start, part), :], sems.at[0])
        )
        copies[-1].start()
        for i in range(width // part):
            cols = slice(i * part, (i + 1) * part)
            buf_a[cols, :] = jnp.where(core == 0, mine[:, cols], theirs[:, cols]).astype(F32)
        copies.append(
            pltpu.make_async_copy(buf_a, grad_in.at[:, pl.ds(start, part)], sems.at[1])
        )
        copies[-1].start()
    if chunk is not None:
        kind = 1 + lax.axis_index("section") % 2
        weight_chunk(kind, core, *factors, *partial, chunk)
    for copy in copies:
        copy.wait()


def add_low(a, b):
    return (a.astype(F32) + b.astype(F32)).astype(BF16)


def outer_kernel(*refs, new, total):
    refs = list(refs)
    del refs[0]
    chip = lax.axis_index("dp") // 2
    new_in = [refs.pop(0)[...] for _ in range(2 * new)]
    total_in = [refs.pop(0)[...] for _ in range(2 * total)]
    values = []
    if new:
        values.append(add_low(*new_in))
        refs.pop(0)[...] = values[-1]
    if total:
        values.append(add_low(*total_in))
        refs.pop(0)[...] = values[-1]
    if new and total:
        middle = jnp.logical_or(chip == 1, chip == 2)
        refs.pop(0)[...] = jnp.where(middle, values[1], values[0])
    token = refs.pop(0)
    token[...] = jnp.zeros_like(token)


def inner_kernel(*refs, inner, final):
    refs = list(refs)
    del refs[0]
    chip = lax.axis_index("dp") // 2
    got = refs.pop(0)[...]
    first = refs.pop(0)[...] if inner else None
    total = refs.pop(0)[...] if final else None
    if inner:
        refs.pop(0)[...] = add_low(first, got)
    if final:
        middle = jnp.logical_or(chip == 1, chip == 2)
        refs.pop(0)[...] = jnp.where(middle, total, got)
    token = refs.pop(0)
    token[...] = jnp.zeros_like(token)


def sum_pages_kernel(token_in, small, total_ref, token, *, group):
    total = small[0:8, :]
    for i in range(8 * group, small.shape[0], 8 * group):
        total += small[i : i + 8, :]
    total_ref[...] = total
    token[...] = jnp.zeros_like(token)


def add_kernel(token_in, a, b, *refs):
    total = a[...] + b[...]
    *outs, token = refs
    token[...] = jnp.zeros_like(token)
    if len(outs) == 1:
        outs[0][...] = total
    else:
        gain, bias, gates = outs
        gain[...] = total[0:1]
        bias[...] = total[1:2]
        gates[...] = total[2:4]


def struct(shape, dtype):
    return jax.ShapeDtypeStruct(shape, dtype)


def params(mebibytes):
    return pltpu.CompilerParams(vmem_limit_bytes=mebibytes << 20)


def in_vmem(*arrays):
    return [pltpu.with_memory_space_constraint(a, pltpu.VMEM) for a in arrays]


def run_load(gain, bias, gates, counts, *arrays):
    width = gain.shape[1]
    inputs = [*arrays, gain, bias, gates, counts.T]
    return pl.pallas_call(
        functools.partial(load_kernel, count=len(arrays)),
        out_shape=[struct((8, width), F32), struct((counts.shape[0], 4 * PAGE), jnp.int32)]
        + [pltpu.VMEM(a.shape, a.dtype) for a in arrays],
        in_specs=[HBM] * len(inputs),
        out_specs=[VMEM] * (2 + len(arrays)),
        scratch_shapes=[
            pltpu.VMEM((1, width), F32),
            pltpu.VMEM((1, width), F32),
            pltpu.VMEM((2, width), F32),
            pltpu.SMEM((2, counts.shape[0]), jnp.int32),
            pltpu.SemaphoreType.DMA((len(inputs),)),
        ],
        compiler_params=params(4),
        name="load_weights",
    )(*[pltpu.with_memory_space_constraint(a, pltpu.HBM) for a in inputs])


def run_forward(tick, limits, incoming, w_in, w_out, vecs, state):
    rows, width = state[0].shape
    hidden = w_in.shape[1]
    return pl.pallas_call(
        functools.partial(forward_kernel, state_in=len(state), tick=tick),
        out_shape=[
            struct(incoming.shape, BF16),
            pltpu.VMEM((rows, width), BF16),
            pltpu.VMEM((rows, width), BF16),
            pltpu.VMEM((rows, hidden), BF16),
            pltpu.VMEM((rows, hidden), BF16),
            pltpu.VMEM((rows, width), F32),
            pltpu.VMEM((rows, 2 * PAGE * (width // (2 * HEAD_DIM))), BF16),
        ],
        in_specs=[VMEM] * (5 + len(state)),
        out_specs=[VMEM] * 7,
        input_output_aliases={5 + i: 1 + i for i in range(len(state))},
        compiler_params=params(12),
        name="forward_page",
    )(limits, incoming, *in_vmem(w_in, w_out), vecs, *state)


def run_backward(tick, sections, incoming, w_in, w_out, vecs, state, back):
    rows, width = back[0].shape
    every = list(state) + list(back)
    return pl.pallas_call(
        functools.partial(
            backward_kernel, state_in=len(every), tick=tick, sections=sections
        ),
        out_shape=[struct(incoming.shape, BF16)]
        + [pltpu.VMEM(s.shape, s.dtype) for s in state]
        + [
            pltpu.VMEM((rows, width), BF16),
            pltpu.VMEM((rows, width), BF16),
            pltpu.VMEM((8 * rows // PAGE, width), F32),
        ],
        in_specs=[VMEM] * (4 + len(every)),
        out_specs=[VMEM] * 10,
        input_output_aliases={4 + i: 1 + i for i in range(len(every))},
        scratch_shapes=[pltpu.VMEM(incoming.shape, BF16)],
        compiler_params=params(12),
        name="backward_page",
    )(incoming, *in_vmem(w_in, w_out), vecs, *every)


TOKEN = (8, 128)


def run_work(token, factors, chunk, totals, place, grads, flush=()):
    width = factors[0].shape[1]
    hidden = factors[1].shape[1]
    part = hidden // CHUNKS
    inputs, specs = [token], [VMEM]
    outs, out_specs, scratch, aliases = [], [], [], {}
    if chunk is not None:
        inputs += in_vmem(*factors)
        specs += [VMEM] * 4
        outs += [struct((part, width), BF16)] * 2
        out_specs += [VMEM] * 2
    if flush:
        inputs += in_vmem(*flush)
        specs += [VMEM] * len(flush)
        outs += [pltpu.HBM(a.shape, a.dtype) for a in flush]
        out_specs += [HBM] * len(flush)
    if place is not None:
        inputs += list(totals)
        specs += [VMEM] * 2
        aliases = {len(inputs) + i: len(outs) + i for i in range(len(grads))}
        inputs += list(grads)
        specs += [HBM] * len(grads)
        outs += [pltpu.HBM((width, hidden), F32), pltpu.HBM((hidden, width), F32)]
        out_specs += [HBM] * 2
        scratch = [
            pltpu.VMEM((width, part), F32),
            pltpu.VMEM((part, width), F32),
            pltpu.SemaphoreType.DMA((2,)),
        ]
    if flush:
        scratch.append(pltpu.SemaphoreType.DMA((len(flush),)))
    *got, token = pl.pallas_call(
        functools.partial(
            work_kernel, chunk=chunk, place=place, placed=len(grads), flush=len(flush)
        ),
        out_shape=outs + [struct(TOKEN, F32)],
        in_specs=specs,
        out_specs=out_specs + [VMEM],
        input_output_aliases=aliases,
        scratch_shapes=scratch,
        compiler_params=params(16),
        name="work_beside",
    )(*inputs)
    made = [got.pop(0) for _ in range(2)] if chunk is not None else None
    flushed = [got.pop(0) for _ in flush]
    return made, (got if place is not None else grads), flushed, token


def run_step(kernel, name, inputs, outs):
    return pl.pallas_call(
        kernel,
        out_shape=[struct(inputs[-1].shape, inputs[-1].dtype)] * outs + [struct(TOKEN, F32)],
        in_specs=[VMEM] * len(inputs),
        out_specs=[VMEM] * (outs + 1),
        compiler_params=params(8),
        name=name,
    )(*inputs)


class SmallSum:
    def __init__(self, small):
        self.small = small
        self.size = lax.axis_size("dp")
        self.step = 0
        self.total = None
        self.got = None

    def advance(self, token):
        if self.step == 0:
            self.total, token = pl.pallas_call(
                functools.partial(sum_pages_kernel, group=GROUP),
                out_shape=[struct((8, self.small.shape[1]), F32), struct(TOKEN, F32)],
                in_specs=[VMEM, VMEM],
                out_specs=[VMEM, VMEM],
                compiler_params=params(4),
                name="small_sum",
            )(token, *in_vmem(self.small))
            self.step = 1
        elif self.got is not None:
            width = self.total.shape[1]
            heights = (8,) if self.step < self.size else (1, 1, 2)
            *outs, token = pl.pallas_call(
                add_kernel,
                out_shape=[struct((h, width), F32) for h in heights] + [struct(TOKEN, F32)],
                in_specs=[VMEM] * 3,
                out_specs=[VMEM] * (len(heights) + 1),
                compiler_params=params(4),
                name="small_sum",
            )(token, self.total, self.got)
            self.total = outs[0] if len(heights) == 1 else outs
            self.got = None
        if self.step < self.size:
            pairs = [(i, i ^ self.step) for i in range(self.size)]
            self.got = lax.ppermute(self.total, "dp", pairs)
            self.step *= 2
        return token

    def done(self):
        return self.step >= self.size and self.got is None


def sum_over_line(token, factors, count, small, flush):
    swap = [(i, i ^ 1) for i in range(8)]
    outer = [(i, i ^ 2) for i in range(8)]
    middle = [(2, 4), (3, 5), (4, 2), (5, 3)]
    lag = LAG
    made, firsts, inners, totals, finals = {}, {}, {}, {}, {}
    got_outer, got_inner = {}, {}
    grads, flushed = (), None

    def work(token, grads, chunk, place, flush=()):
        chunk = chunk if chunk is not None and chunk < count else None
        place = place if place is not None and 0 <= place < count else None
        if chunk is None and place is None:
            return token, grads, ()
        pair = finals.pop(place) if place is not None else None
        new, grads, flushed, token = run_work(token, factors, chunk, pair, place, grads, flush)
        if new:
            made[chunk] = (new[0], lax.ppermute(new[1], "dp", swap))
        return token, grads, flushed

    for k in range(AHEAD):
        token, grads, _ = work(token, grads, k, None)

    def at(half, stage):
        k, odd = divmod(half - stage * lag, 2)
        return k if not odd and 0 <= k < count else None

    for half in range(2 * count - 1 + 3 * lag):
        if half % 2 == 0:
            new, total = at(half, 0), at(half, 2)
            inputs = [token]
            if new is not None:
                inputs += made.pop(new)
            if total is not None:
                inputs += [inners.pop(total), got_inner.pop(half - lag)]
            if len(inputs) > 1:
                both = new is not None and total is not None
                kernel = functools.partial(
                    outer_kernel, new=int(new is not None), total=int(total is not None)
                )
                *outs, token = run_step(kernel, "outer_step", inputs, 2 + 1 if both else 1)
                send = outs[-1]
                if new is not None:
                    firsts[new] = outs[0]
                if total is not None:
                    totals[total] = outs[1 if both else 0]
                got_outer[half] = lax.ppermute(send, "dp", outer)
            if not small.done() and half >= 4 and half % 4 == 0:
                token = small.advance(token)
        else:
            inner, final = at(half, 1), at(half, 3)
            if inner is not None or final is not None:
                inputs = [token, got_outer.pop(half - lag)]
                if inner is not None:
                    inputs.append(firsts.pop(inner))
                if final is not None:
                    inputs.append(totals.pop(final))
                kernel = functools.partial(
                    inner_kernel, inner=inner is not None, final=final is not None
                )
                *outs, token = run_step(
                    kernel, "inner_step", inputs, (inner is not None) + (final is not None)
                )
                if inner is not None:
                    inners[inner] = outs[0]
                    got_inner[half] = lax.ppermute(outs[0], "dp", middle)
                if final is not None:
                    finals[final] = (outs[-1], lax.ppermute(outs[-1], "dp", swap))
            chunk = (half - 1) // 2 + AHEAD
            place = at(half - 2, 3)
            token, grads, rows = work(token, grads, chunk, place, flush if half == 1 else ())
            flushed = rows or flushed
    token, grads, _ = work(token, grads, None, count - 1)
    while not small.done():
        token = small.advance(token)
    return grads, flushed


def body(acts, cotan, counts, weight_in, weight_out, ln_gain, ln_bias, gate_vec):
    sections = lax.axis_size("section")
    dp_index = lax.axis_index("dp")
    dp_size = lax.axis_size("dp")
    rows, width = acts.shape
    micros = rows // (GROUP * PAGE)
    vecs, limits, w_in, w_out, acts, cotan = run_load(
        ln_gain, ln_bias, gate_vec[0], counts, weight_in[0], weight_out[0], acts, cotan
    )
    incoming = jnp.zeros((GROUP * PAGE, width), BF16)
    core = dp_index % 2
    empty = incoming
    state, back = (acts,), (cotan,)
    upstream = {}
    for tick in range(micros + (1 + BACK_LAG) * (sections - 1)):
        if tick < micros + sections - 1:
            y, *state = run_forward(tick, limits, incoming, w_in, w_out, vecs, state)
            pairs = [(a, a + 1) for a in range(sections - 1) if 0 <= tick - a < micros]
            if pairs:
                incoming = lax.ppermute(y, "section", pairs)
        slot = tick - (sections - 1)
        if slot >= 0:
            dx, *both = run_backward(
                slot, sections, upstream.pop(slot, empty), w_in, w_out, vecs, state, back
            )
            state, back = both[:6], both[6:]
            pairs = [
                (a, a - 1)
                for a in range(1, sections)
                if 0 <= slot - BACK_LAG * (sections - 1 - a) < micros
            ]
            if pairs:
                upstream[slot + BACK_LAG] = lax.ppermute(dx, "section", pairs)
    xin, outputs, sav, dh, *_ = state
    grads, db, small = back
    factors = (xin, sav, dh, db)
    small = SmallSum(small)
    token = jnp.zeros(TOKEN, F32)
    if dp_size == 8:
        (grad_in, grad_out), (outputs, grads) = sum_over_line(
            token, factors, CHUNKS, small, (outputs, grads)
        )
    else:
        so_far = ()
        for k in range(CHUNKS):
            (own, other), _, _, token = run_work(token, factors, k, None, None, ())
            pair = jnp.where(core == 0, jnp.stack([own, other]), jnp.stack([other, own]))
            pair = lax.psum(pair, "dp")
            pair = jnp.where(core == 0, pair, pair[::-1])
            _, so_far, _, token = run_work(
                token, factors, None, (pair[0], pair[1]), k, so_far
            )
        grad_in, grad_out = so_far
        while not small.done():
            token = small.advance(token)
    grad_gain, grad_bias, grad_gate = small.total
    return (
        outputs[None],
        grads[None],
        grad_in[None],
        grad_out[None],
        grad_gain,
        grad_bias,
        grad_gate[None],
    )


def solution(mesh):
    return jax.shard_map(
        body,
        mesh=mesh,
        in_specs=(
            P("dp", None),
            P("dp", None),
            P("dp", None),
            P("section", None, None),
            P("section", None, None),
            P("section", None),
            P("section", None),
            P("section", None, None),
        ),
        out_specs=(
            P("section", "dp", None),
            P("section", "dp", None),
            P("section", None, None),
            P("section", None, None),
            P("section", None),
            P("section", None),
            P("section", None, None),
        ),
        check_vma=False,
    )
```

```python
import functools

import jax
import jax.numpy as jnp
from jax import lax
from jax.experimental import pallas as pl
from jax.experimental.pallas import tpu as pltpu
from jax.sharding import PartitionSpec as P

HEAD_DIM = 64
VIS = 16
TXT = 112
PAGE = VIS + TXT
SCORE_SCALE = 0.125
MASK_FILL = -1e30
CHUNKS = 12
LAG = 3
AHEAD = 2
TOGETHER = 6
BACK_LAG = 1
FORWARD = (2, 2, 2, 2)
BACKWARD = (2, 2, 2, 2)
GELU_A = 0.7978845608028654
GELU_B = 0.044715
F32 = jnp.float32
BF16 = jnp.bfloat16

VMEM = pl.BlockSpec(memory_space=pltpu.VMEM)
SMEM = pl.BlockSpec(memory_space=pltpu.SMEM)
HBM = pl.BlockSpec(memory_space=pltpu.HBM)


def dot(a, b):
    return jnp.dot(a, b, preferred_element_type=F32)


def dot_nt(a, b):
    return lax.dot_general(a, b, (((1,), (1,)), ((), ())), preferred_element_type=F32)


def dot_tn(a, b):
    return lax.dot_general(a, b, (((0,), (0,)), ((), ())), preferred_element_type=F32)


def text_of(value):
    pages = [value[i + VIS : i + PAGE] for i in range(0, value.shape[0], PAGE)]
    return pages[0] if len(pages) == 1 else jnp.concatenate(pages, axis=0)


def visual_of(value):
    pages = [value[i : i + VIS] for i in range(0, value.shape[0], PAGE)]
    return pages[0] if len(pages) == 1 else jnp.concatenate(pages, axis=0)


def to_pages(visual, text):
    pieces = []
    for i in range(visual.shape[0] // VIS):
        pieces += [visual[i * VIS : (i + 1) * VIS], text[i * TXT : (i + 1) * TXT]]
    return jnp.concatenate(pieces, axis=0)


def gate_table(vecs, rows, width):
    visual = lax.broadcasted_iota(jnp.int32, (rows, width), 0) % PAGE < VIS
    return jnp.where(visual, vecs[3:4, :], vecs[2:3, :])


def tail_parts(x, branch, gate_rows):
    gate = jax.nn.sigmoid(jnp.sum(x * gate_rows, axis=-1, keepdims=True))
    mixed = x + gate * branch
    centred = mixed - jnp.mean(mixed, axis=-1, keepdims=True)
    inv = lax.rsqrt(jnp.mean(centred * centred, axis=-1, keepdims=True) + 1e-05)
    return gate, centred * inv, inv


def allowed_pairs(limit_row, cross):
    key = lax.broadcasted_iota(jnp.int32, (PAGE, 2 * PAGE), 0)
    query = lax.broadcasted_iota(jnp.int32, (PAGE, 2 * PAGE), 1) % PAGE
    limit = jnp.where(key < VIS, limit_row[:, : 2 * PAGE], limit_row[:, 2 * PAGE :])
    unlike = jnp.where(query < VIS, 1, 0) + jnp.where(key < VIS, 1, 0) - 1
    return key + (PAGE * cross) * (unlike * unlike) < limit


def low_lanes(shape):
    return lax.broadcasted_iota(jnp.int32, shape, 1) < HEAD_DIM


def stack_heads(pair):
    low = low_lanes(pair.shape)
    zero = jnp.zeros_like(pair)
    return jnp.concatenate([jnp.where(low, pair, zero), jnp.where(low, zero, pair)], axis=0)


def unstack_heads(stacked):
    half = stacked.shape[0] // 2
    top = stacked[:half]
    return jnp.where(low_lanes(top.shape), top, stacked[half:])


def masked_softmax(scores, allowed):
    scores = jnp.where(allowed, scores * SCORE_SCALE, MASK_FILL)
    weights = jnp.exp(scores - jnp.max(scores, axis=0, keepdims=True))
    return weights / jnp.sum(weights, axis=0, keepdims=True)


def load_kernel(*refs, count):
    sources, live_in = refs[: count + 3], refs[count + 3]
    vecs, limits = refs[count + 4 : count + 6]
    targets = refs[count + 6 : 2 * count + 6]
    gain, bias, gates, live, sems = refs[2 * count + 6 :]
    targets = (*targets, gain, bias, gates)
    copies = [
        pltpu.make_async_copy(source, target, sems.at[i])
        for i, (source, target) in enumerate(zip(sources, targets))
    ]
    live_copy = pltpu.make_async_copy(live_in, live, sems.at[count + 3])
    for copy in copies[count:] + [live_copy] + copies[:count]:
        copy.start()
    for copy in copies[count:] + [live_copy]:
        copy.wait()
    vecs[0:1, :] = gain[...]
    vecs[1:2, :] = bias[...]
    vecs[2:4, :] = gates[...]
    first = lax.broadcasted_iota(jnp.int32, (1, 4 * PAGE), 1) < 2 * PAGE
    for page in range(limits.shape[0]):
        limits[page : page + 1, :] = jnp.where(first, live[0, page], live[1, page] + VIS)
    for copy in copies[:count]:
        copy.wait()


def block(index, size):
    if isinstance(index, int):
        return slice(index * size, (index + 1) * size)
    return pl.ds(pl.multiple_of(index * size, size), size)


def page_rows(first_page, i):
    return pl.ds(pl.multiple_of((first_page + i) * PAGE, PAGE), PAGE)


def each_group(plan, section, run):
    groups = {}
    for s, (page, size) in plan.items():
        groups.setdefault((s % 2, size), []).append((s, page))
    for (odd, size), members in groups.items():
        here, first = section == members[0][0], members[0][1]
        for s, page in members[1:]:
            here = jnp.logical_or(here, section == s)
            first = jnp.where(section == s, page, first)

        @pl.when(here)
        def _():
            run(odd == 0, first, size * PAGE)


def forward_kernel(limits, w_in, w_out, vecs, *refs, state_in, plan, sizes_in, sizes_out):
    incoming = dict(zip(sizes_in, refs))
    refs = refs[len(sizes_in) + state_in :]
    outgoing = dict(zip(sizes_out, refs))
    state = refs[len(sizes_out) :]
    section = lax.axis_index("section")

    def run(is_attention, page, micro):
        size = micro // PAGE
        part = (limits, incoming.get(size), w_in, w_out, vecs, outgoing.get(size), *state)
        forward_part(*part, section, page, micro, is_attention)

    each_group(plan, section, run)


def forward_part(
    limits, incoming, w_in, w_out, vecs, y_ref, xin, out, sav, dh, br, probs_ref,
    section, page, micro, is_attention,
):
    width = xin.shape[1]
    group = micro // PAGE
    cross = jnp.where(section == 0, 1, 0)
    rows = pl.ds(pl.multiple_of(page * PAGE, PAGE), micro)

    def begin():
        x_low = xin[rows, :]
        if incoming is not None:
            x_low = jnp.where(section == 0, x_low, incoming[...])
        xin[rows, :] = x_low
        return x_low

    def finish(x_low, branch):
        br[rows, :] = branch
        gate, normed, inv = tail_parts(
            x_low.astype(F32), branch, gate_table(vecs, micro, width)
        )
        y = (normed * vecs[0:1, :] + vecs[1:2, :]).astype(BF16)
        if y_ref is not None:
            y_ref[...] = y
        out[rows, :] = y

    def attention():
        x_low = begin()
        x_text, x_visual = text_of(x_low), visual_of(x_low)

        for k in range(3):
            cols = block(k, width)
            sav[rows, cols] = to_pages(
                dot(x_visual, w_out[cols, :]).astype(BF16), dot(x_text, w_in[:, cols]).astype(BF16)
            )

        for i in range(group):
            here = page_rows(page, i)
            allowed = allowed_pairs(limits[pl.ds(page + i, 1), :], cross)
            pairs = width // (2 * HEAD_DIM)

            for first in range(0, pairs, TOGETHER):
                some = range(first, first + TOGETHER)
                scores = [
                    dot_nt(
                        sav[here, block(pairs + n, 128)],
                        stack_heads(sav[here, block(n, 128)]),
                    )
                    for n in some
                ]
                probs = [masked_softmax(one, allowed).astype(BF16) for one in scores]
                contexts = [
                    dot_tn(one, sav[here, block(2 * pairs + n, 128)])
                    for n, one in zip(some, probs)
                ]
                for n, one, context in zip(some, probs, contexts):
                    probs_ref[here, block(n, 2 * PAGE)] = one
                    sav[here, block(3 * pairs + n, 128)] = unstack_heads(context).astype(BF16)

        context = sav[rows, 3 * width :]
        finish(
            x_low,
            to_pages(
                dot(visual_of(context), w_out[3 * width :, :]),
                dot(text_of(context), w_in[:, 3 * width :]),
            ),
        )

    def feed():
        x_low = begin()

        hidden_width = w_in.shape[1]
        branch = None
        ahead = dot(x_low, w_in[:, :width])
        for start in range(0, hidden_width, width):
            cols = slice(start, start + width)
            hidden = ahead
            if start + width < hidden_width:
                ahead = dot(x_low, w_in[:, start + width : start + 2 * width])
            square = hidden * hidden
            tanh = jnp.tanh(hidden * (GELU_A + (GELU_A * GELU_B) * square))
            half = 0.5 + 0.5 * tanh
            active = hidden * half
            low = active.astype(BF16)
            sav[rows, cols] = low
            slope = half + (active * (1.0 - tanh)) * (
                GELU_A + (3.0 * GELU_A * GELU_B) * square
            )
            dh[rows, cols] = slope.astype(BF16)
            part = dot(low, w_out[cols, :])
            branch = part if branch is None else branch + part
        finish(x_low, branch)

    (attention if is_attention else feed)()


def backward_kernel(
    w_in, w_out, vecs, *refs, state_in, plan, sizes_in, sizes_out, sections, phase
):
    incoming = dict(zip(sizes_in, refs))
    late = phase == "rest"
    refs = refs[len(sizes_in) + late + state_in :]
    outgoing = dict(zip(sizes_out, refs))
    state, dc = refs[len(sizes_out) : -1 - late], refs[-1]
    if late:
        refs[-2][...] = jnp.zeros_like(refs[-2])
    section = lax.axis_index("section")

    def run(is_attention, page, micro):
        size = micro // PAGE
        part = (incoming.get(size), w_in, w_out, vecs, outgoing.get(size), *state, dc)
        backward_part(*part, section == sections - 1, page, micro, is_attention, phase)

    each_group(plan, section, run)


def backward_part(
    incoming, w_in, w_out, vecs, dx_ref, xin, out, sav, dh, br, probs_ref, grads, db, small, dc,
    is_last, page, micro, is_attention, phase,
):
    width = xin.shape[1]
    group = micro // PAGE
    rows = pl.ds(pl.multiple_of(page * PAGE, PAGE), micro)

    def tail():
        x = xin[rows, :].astype(F32)
        branch = br[rows, :]
        gate_rows = gate_table(vecs, micro, width)
        gate, normed, inv = tail_parts(x, branch, gate_rows)
        dy = grads[rows, :]
        if incoming is not None:
            dy = jnp.where(is_last, dy, incoming[...])
        dy = dy.astype(F32)
        dn = dy * vecs[0:1, :]
        du = inv * (
            dn
            - jnp.mean(dn, axis=-1, keepdims=True)
            - normed * jnp.mean(dn * normed, axis=-1, keepdims=True)
        )
        dbranch = (du * gate).astype(BF16)
        db[rows, :] = dbranch
        dz = jnp.sum(du * branch, axis=-1, keepdims=True) * gate * (1.0 - gate)
        weighted = dz * x
        sums = jnp.concatenate(
            [
                jnp.sum(dy * normed, axis=0, keepdims=True),
                jnp.sum(dy, axis=0, keepdims=True),
                jnp.sum(text_of(weighted), axis=0, keepdims=True),
                jnp.sum(visual_of(weighted), axis=0, keepdims=True),
                jnp.zeros((4, width), F32),
            ],
            axis=0,
        )
        small[pl.ds(pl.multiple_of(page * 8, 8), 8), :] = sums
        for i in range(1, group):
            small[pl.ds(pl.multiple_of((page + i) * 8, 8), 8), :] = jnp.zeros_like(sums)
        br[rows, :] = du + dz * gate_rows

    def finish(total):
        dx = total.astype(BF16)
        if dx_ref is not None:
            dx_ref[...] = dx
        grads[rows, :] = dx

    def attention():
        if phase != "rest":
            tail()
        if phase == "tail":
            return
        dbranch = db[rows, :]
        dc[:micro, :] = to_pages(
            dot_nt(visual_of(dbranch), w_out[3 * width :, :]).astype(BF16),
            dot_nt(text_of(dbranch), w_in[:, 3 * width :]).astype(BF16),
        )
        for i in range(group):
            here = page_rows(page, i)
            own = slice(i * PAGE, (i + 1) * PAGE)
            pairs = width // (2 * HEAD_DIM)

            for first in range(0, pairs, TOGETHER):
                some = range(first, first + TOGETHER)
                contexts = [stack_heads(dc[own, block(n, 128)]) for n in some]
                dprobs = [
                    dot_nt(sav[here, block(2 * pairs + n, 128)], one)
                    for n, one in zip(some, contexts)
                ]
                low = [probs_ref[here, block(n, 2 * PAGE)] for n in some]
                dvalues = [dot(one, context) for one, context in zip(low, contexts)]
                dscores = []
                for one, change in zip(low, dprobs):
                    probs = one.astype(F32)
                    mean = jnp.sum(change * probs, axis=0, keepdims=True)
                    dscores.append((probs * (change - mean)).astype(BF16))
                dkeys = [
                    dot(one, stack_heads(sav[here, block(n, 128)]))
                    for n, one in zip(some, dscores)
                ]
                dqueries = [
                    dot_tn(one, sav[here, block(pairs + n, 128)])
                    for n, one in zip(some, dscores)
                ]
                for n, dquery, dkey, dvalue in zip(some, dqueries, dkeys, dvalues):
                    dh[here, block(2 * pairs + n, 128)] = dvalue.astype(BF16)
                    dh[here, block(pairs + n, 128)] = (dkey * SCORE_SCALE).astype(BF16)
                    dh[here, block(n, 128)] = (unstack_heads(dquery) * SCORE_SCALE).astype(BF16)

        text, visual = None, None
        for k in range(3):
            cols = slice(k * width, (k + 1) * width)
            part = dh[rows, cols]
            one = dot_nt(text_of(part), w_in[:, cols])
            two = dot_nt(visual_of(part), w_out[cols, :])
            text = one if text is None else text + one
            visual = two if visual is None else visual + two
        finish(br[rows, :] + to_pages(visual, text))

    def feed():
        if phase != "rest":
            tail()
        if phase == "tail":
            return
        dbranch, total = db[rows, :], br[rows, :]
        for start in range(0, w_in.shape[1], width):
            cols = slice(start, start + width)
            dhidden = (dot_nt(dbranch, w_out[cols, :]) * dh[rows, cols].astype(F32)).astype(BF16)
            dh[rows, cols] = dhidden
            total = total + dot_nt(dhidden, w_in[:, cols])
        finish(total)

    (attention if is_attention else feed)()


def weight_chunk(kind, core, xin, sav, dh, db, own_ref, other_ref, chunk):
    part, width = own_ref.shape
    start = chunk * part
    cols = slice(start, start + part)

    def put(grad_a, grad_b):
        low_a = jnp.concatenate(
            [grad_a[i : i + part].astype(BF16) for i in range(0, width, part)], axis=1
        )
        low_b = grad_b.astype(BF16)
        own_ref[...] = jnp.where(core == 0, low_a, low_b)
        other_ref[...] = jnp.where(core == 0, low_b, low_a)

    @pl.when(kind == 1)
    def attention():
        block, inner = start // width, start % width
        inner_cols = slice(inner, inner + part)
        if block < 3:
            left, right = xin[...], dh[:, block * width : (block + 1) * width]
            put(
                dot_tn(text_of(left), text_of(dh[:, cols])),
                dot_tn(visual_of(left[:, inner_cols]), visual_of(right)),
            )
        else:
            left, right = sav[:, 3 * width :], db[...]
            put(
                dot_tn(text_of(left), text_of(right[:, inner_cols])),
                dot_tn(visual_of(left[:, inner_cols]), visual_of(right)),
            )

    @pl.when(kind == 2)
    def feed():
        put(dot_tn(xin[...], dh[:, cols]), dot_tn(sav[:, cols], db[...]))


def work_kernel(*refs, chunk, place, placed, flush):
    refs = list(refs)
    del refs[0]
    core = lax.axis_index("dp") % 2

    def take(count):
        taken = refs[:count]
        del refs[:count]
        return taken

    factors = take(4) if chunk is not None else None
    rows_in = take(flush)
    if place is not None:
        own, other = take(2)
        take(placed)
    partial = take(2) if chunk is not None else None
    rows_out = take(flush)
    if place is not None:
        grad_in, grad_out = take(2)
    (token,) = take(1)
    token[...] = jnp.zeros_like(token)
    copies = []
    if flush:
        row_sems = refs.pop()
        for i, (source, target) in enumerate(zip(rows_in, rows_out)):
            copies.append(pltpu.make_async_copy(source, target, row_sems.at[i]))
            copies[-1].start()
    if place is not None:
        buf_a, buf_b, sems = refs
        part, width = buf_b.shape
        start = place * part
        mine, theirs = own[...], other[...]
        buf_b[...] = jnp.where(core == 0, theirs, mine).astype(F32)
        copies.append(
            pltpu.make_async_copy(buf_b, grad_out.at[pl.ds(start, part), :], sems.at[0])
        )
        copies[-1].start()
        for i in range(width // part):
            cols = slice(i * part, (i + 1) * part)
            buf_a[cols, :] = jnp.where(core == 0, mine[:, cols], theirs[:, cols]).astype(F32)
        copies.append(
            pltpu.make_async_copy(buf_a, grad_in.at[:, pl.ds(start, part)], sems.at[1])
        )
        copies[-1].start()
    if chunk is not None:
        kind = 1 + lax.axis_index("section") % 2
        weight_chunk(kind, core, *factors, *partial, chunk)
    for copy in copies:
        copy.wait()


def add_low(a, b):
    return (a.astype(F32) + b.astype(F32)).astype(BF16)


def outer_kernel(*refs, new, total):
    refs = list(refs)
    del refs[0]
    chip = lax.axis_index("dp") // 2
    new_in = [refs.pop(0)[...] for _ in range(2 * new)]
    total_in = [refs.pop(0)[...] for _ in range(2 * total)]
    values = []
    if new:
        values.append(add_low(*new_in))
        refs.pop(0)[...] = values[-1]
    if total:
        values.append(add_low(*total_in))
        refs.pop(0)[...] = values[-1]
    if new and total:
        middle = jnp.logical_or(chip == 1, chip == 2)
        refs.pop(0)[...] = jnp.where(middle, values[1], values[0])
    token = refs.pop(0)
    token[...] = jnp.zeros_like(token)


def inner_kernel(*refs, inner, final):
    refs = list(refs)
    del refs[0]
    chip = lax.axis_index("dp") // 2
    got = refs.pop(0)[...]
    first = refs.pop(0)[...] if inner else None
    total = refs.pop(0)[...] if final else None
    if inner:
        refs.pop(0)[...] = add_low(first, got)
    if final:
        middle = jnp.logical_or(chip == 1, chip == 2)
        refs.pop(0)[...] = jnp.where(middle, total, got)
    token = refs.pop(0)
    token[...] = jnp.zeros_like(token)


def sum_pages_kernel(token_in, small, total_ref, token):
    total = small[0:8, :]
    for i in range(8, small.shape[0], 8):
        total += small[i : i + 8, :]
    total_ref[...] = total
    token[...] = jnp.zeros_like(token)


def add_kernel(token_in, a, b, *refs):
    total = a[...] + b[...]
    *outs, token = refs
    token[...] = jnp.zeros_like(token)
    if len(outs) == 1:
        outs[0][...] = total
    else:
        gain, bias, gates = outs
        gain[...] = total[0:1]
        bias[...] = total[1:2]
        gates[...] = total[2:4]


def struct(shape, dtype):
    return jax.ShapeDtypeStruct(shape, dtype)


def params(mebibytes):
    return pltpu.CompilerParams(vmem_limit_bytes=mebibytes << 20)


def in_vmem(*arrays):
    return [pltpu.with_memory_space_constraint(a, pltpu.VMEM) for a in arrays]


def run_load(gain, bias, gates, counts, *arrays):
    width = gain.shape[1]
    inputs = [*arrays, gain, bias, gates, counts.T]
    return pl.pallas_call(
        functools.partial(load_kernel, count=len(arrays)),
        out_shape=[struct((8, width), F32), struct((counts.shape[0], 4 * PAGE), jnp.int32)]
        + [pltpu.VMEM(a.shape, a.dtype) for a in arrays],
        in_specs=[HBM] * len(inputs),
        out_specs=[VMEM] * (2 + len(arrays)),
        scratch_shapes=[
            pltpu.VMEM((1, width), F32),
            pltpu.VMEM((1, width), F32),
            pltpu.VMEM((2, width), F32),
            pltpu.SMEM((2, counts.shape[0]), jnp.int32),
            pltpu.SemaphoreType.DMA((len(inputs),)),
        ],
        compiler_params=params(4),
        name="load_weights",
    )(*[pltpu.with_memory_space_constraint(a, pltpu.HBM) for a in inputs])


def run_forward(plan, limits, incoming, sizes_out, w_in, w_out, vecs, state):
    rows, width = state[0].shape
    hidden = w_in.shape[1]
    sizes_in = tuple(incoming)
    first = 4 + len(sizes_in)
    got = pl.pallas_call(
        functools.partial(
            forward_kernel,
            state_in=len(state), plan=plan, sizes_in=sizes_in, sizes_out=sizes_out,
        ),
        out_shape=[struct((size * PAGE, width), BF16) for size in sizes_out]
        + [
            pltpu.VMEM((rows, width), BF16),
            pltpu.VMEM((rows, width), BF16),
            pltpu.VMEM((rows, hidden), BF16),
            pltpu.VMEM((rows, hidden), BF16),
            pltpu.VMEM((rows, width), F32),
            pltpu.VMEM((rows, 2 * PAGE * (width // (2 * HEAD_DIM))), BF16),
        ],
        in_specs=[VMEM] * (first + len(state)),
        out_specs=[VMEM] * (len(sizes_out) + 6),
        input_output_aliases={first + i: len(sizes_out) + i for i in range(len(state))},
        compiler_params=params(12),
        name="forward_pages",
    )(limits, *in_vmem(w_in, w_out), vecs, *incoming.values(), *state)
    return dict(zip(sizes_out, got)), got[len(sizes_out) :]


def run_backward(
    plan, incoming, sizes_out, sections, w_in, w_out, vecs, state, back, phase=None, token=None
):
    rows, width = back[0].shape
    every = list(state) + list(back)
    sizes_in = tuple(incoming)
    late = [] if token is None else [token]
    first = 3 + len(sizes_in) + len(late)
    largest = max(size for _, size in plan.values())
    got = pl.pallas_call(
        functools.partial(
            backward_kernel,
            state_in=len(every), plan=plan, sizes_in=sizes_in, sizes_out=sizes_out,
            sections=sections, phase=phase,
        ),
        out_shape=[struct((size * PAGE, width), BF16) for size in sizes_out]
        + [pltpu.VMEM(s.shape, s.dtype) for s in state]
        + [
            pltpu.VMEM((rows, width), BF16),
            pltpu.VMEM((rows, width), BF16),
            pltpu.VMEM((8 * rows // PAGE, width), F32),
        ]
        + [struct(TOKEN, F32) for _ in late],
        in_specs=[VMEM] * (first + len(every)),
        out_specs=[VMEM] * (len(sizes_out) + 9 + len(late)),
        input_output_aliases={first + i: len(sizes_out) + i for i in range(len(every))},
        scratch_shapes=[pltpu.VMEM((largest * PAGE, width), BF16)],
        compiler_params=params(12),
        name="backward_pages",
    )(*in_vmem(w_in, w_out), vecs, *incoming.values(), *late, *every)
    state_out = got[len(sizes_out) :]
    return dict(zip(sizes_out, got)), state_out[:6], state_out[6:9], *state_out[9:]


def send_pages(values, plan, step, sections):
    sent = {}
    for size, value in values.items():
        pairs = [
            (s, s + step)
            for s, (_, own) in plan.items()
            if own == size and 0 <= s + step < sections
        ]
        sent[size] = lax.ppermute(value, "section", pairs)
    return sent


def micro_batches(sizes, pages):
    if sum(sizes) != pages:
        sizes = (1,) * pages
    starts = [sum(sizes[:i]) for i in range(len(sizes))]
    return list(zip(starts, sizes))


TOKEN = (8, 128)


def run_work(token, factors, chunk, totals, place, grads, flush=()):
    width = factors[0].shape[1]
    hidden = factors[1].shape[1]
    part = hidden // CHUNKS
    inputs, specs = [token], [VMEM]
    outs, out_specs, scratch, aliases = [], [], [], {}
    if chunk is not None:
        inputs += in_vmem(*factors)
        specs += [VMEM] * 4
        outs += [struct((part, width), BF16)] * 2
        out_specs += [VMEM] * 2
    if flush:
        inputs += in_vmem(*flush)
        specs += [VMEM] * len(flush)
        outs += [pltpu.HBM(a.shape, a.dtype) for a in flush]
        out_specs += [HBM] * len(flush)
    if place is not None:
        inputs += list(totals)
        specs += [VMEM] * 2
        aliases = {len(inputs) + i: len(outs) + i for i in range(len(grads))}
        inputs += list(grads)
        specs += [HBM] * len(grads)
        outs += [pltpu.HBM((width, hidden), F32), pltpu.HBM((hidden, width), F32)]
        out_specs += [HBM] * 2
        scratch = [
            pltpu.VMEM((width, part), F32),
            pltpu.VMEM((part, width), F32),
            pltpu.SemaphoreType.DMA((2,)),
        ]
    if flush:
        scratch.append(pltpu.SemaphoreType.DMA((len(flush),)))
    *got, token = pl.pallas_call(
        functools.partial(
            work_kernel, chunk=chunk, place=place, placed=len(grads), flush=len(flush)
        ),
        out_shape=outs + [struct(TOKEN, F32)],
        in_specs=specs,
        out_specs=out_specs + [VMEM],
        input_output_aliases=aliases,
        scratch_shapes=scratch,
        compiler_params=params(16),
        name="work_beside",
    )(*inputs)
    made = [got.pop(0) for _ in range(2)] if chunk is not None else None
    flushed = [got.pop(0) for _ in flush]
    return made, (got if place is not None else grads), flushed, token


def run_step(kernel, name, inputs, outs):
    return pl.pallas_call(
        kernel,
        out_shape=[struct(inputs[-1].shape, inputs[-1].dtype)] * outs + [struct(TOKEN, F32)],
        in_specs=[VMEM] * len(inputs),
        out_specs=[VMEM] * (outs + 1),
        compiler_params=params(8),
        name=name,
    )(*inputs)


class SmallSum:
    def __init__(self, small):
        self.small = small
        self.size = lax.axis_size("dp")
        self.step = 0
        self.total = None
        self.got = None

    def advance(self, token):
        if self.step == 0:
            self.total, token = pl.pallas_call(
                sum_pages_kernel,
                out_shape=[struct((8, self.small.shape[1]), F32), struct(TOKEN, F32)],
                in_specs=[VMEM, VMEM],
                out_specs=[VMEM, VMEM],
                compiler_params=params(4),
                name="small_sum",
            )(token, *in_vmem(self.small))
            self.step = 1
        elif self.got is not None:
            width = self.total.shape[1]
            heights = (8,) if self.step < self.size else (1, 1, 2)
            *outs, token = pl.pallas_call(
                add_kernel,
                out_shape=[struct((h, width), F32) for h in heights] + [struct(TOKEN, F32)],
                in_specs=[VMEM] * 3,
                out_specs=[VMEM] * (len(heights) + 1),
                compiler_params=params(4),
                name="small_sum",
            )(token, self.total, self.got)
            self.total = outs[0] if len(heights) == 1 else outs
            self.got = None
        if self.step < self.size:
            pairs = [(i, i ^ self.step) for i in range(self.size)]
            self.got = lax.ppermute(self.total, "dp", pairs)
            self.step *= 2
        return token

    def done(self):
        return self.step >= self.size and self.got is None


def sum_over_line(token, factors, late):
    count = CHUNKS
    order = [(k + count * 3 // 4) % count for k in range(count)]
    small, flush = None, ()
    swap = [(i, i ^ 1) for i in range(8)]
    outer = [(i, i ^ 2) for i in range(8)]
    middle = [(2, 4), (3, 5), (4, 2), (5, 3)]
    lag = LAG
    made, firsts, inners, totals, finals = {}, {}, {}, {}, {}
    got_outer, got_inner = {}, {}
    grads, flushed = (), None

    def work(token, grads, chunk, place, flush=()):
        chunk = chunk if chunk is not None and chunk < count else None
        place = place if place is not None and 0 <= place < count else None
        if chunk is None and place is None:
            return token, grads, ()
        pair = finals.pop(place) if place is not None else None
        new, grads, flushed, token = run_work(
            token,
            factors,
            None if chunk is None else order[chunk],
            pair,
            None if place is None else order[place],
            grads,
            flush,
        )
        if new:
            made[chunk] = (new[0], lax.ppermute(new[1], "dp", swap))
        return token, grads, flushed

    for k in range(AHEAD):
        token, grads, _ = work(token, grads, k, None)

    def at(half, stage):
        k, odd = divmod(half - stage * lag, 2)
        return k if not odd and 0 <= k < count else None

    for half in range(2 * count - 1 + 3 * lag):
        if half % 2 == 0:
            new, total = at(half, 0), at(half, 2)
            inputs = [token]
            if new is not None:
                inputs += made.pop(new)
            if total is not None:
                inputs += [inners.pop(total), got_inner.pop(half - lag)]
            if len(inputs) > 1:
                both = new is not None and total is not None
                kernel = functools.partial(
                    outer_kernel, new=int(new is not None), total=int(total is not None)
                )
                *outs, token = run_step(kernel, "outer_step", inputs, 2 + 1 if both else 1)
                send = outs[-1]
                if new is not None:
                    firsts[new] = outs[0]
                if total is not None:
                    totals[total] = outs[1 if both else 0]
                got_outer[half] = lax.ppermute(send, "dp", outer)
            if half == 2:
                (factors, flush, rows), token = late(token)
                small = SmallSum(rows)
            if half >= 4 and half % 4 == 0 and not small.done():
                token = small.advance(token)
        else:
            inner, final = at(half, 1), at(half, 3)
            if inner is not None or final is not None:
                inputs = [token, got_outer.pop(half - lag)]
                if inner is not None:
                    inputs.append(firsts.pop(inner))
                if final is not None:
                    inputs.append(totals.pop(final))
                kernel = functools.partial(
                    inner_kernel, inner=inner is not None, final=final is not None
                )
                *outs, token = run_step(
                    kernel, "inner_step", inputs, (inner is not None) + (final is not None)
                )
                if inner is not None:
                    inners[inner] = outs[0]
                    got_inner[half] = lax.ppermute(outs[0], "dp", middle)
                if final is not None:
                    finals[final] = (outs[-1], lax.ppermute(outs[-1], "dp", swap))
            chunk = (half - 1) // 2 + AHEAD
            place = at(half - 2, 3)
            token, grads, rows = work(token, grads, chunk, place, flush if half == 3 else ())
            flushed = rows or flushed
    token, grads, _ = work(token, grads, None, count - 1)
    while not small.done():
        token = small.advance(token)
    return grads, flushed, small


def body(acts, cotan, counts, weight_in, weight_out, ln_gain, ln_bias, gate_vec):
    sections = lax.axis_size("section")
    dp_index = lax.axis_index("dp")
    dp_size = lax.axis_size("dp")
    rows, width = acts.shape
    vecs, limits, w_in, w_out, acts, cotan = run_load(
        ln_gain, ln_bias, gate_vec[0], counts, weight_in[0], weight_out[0], acts, cotan
    )
    core = dp_index % 2
    ahead = micro_batches(FORWARD, rows // PAGE)
    behind = micro_batches(BACKWARD, rows // PAGE)
    last = sections - 1
    state, back = (acts,), (cotan,)
    incoming, upstream = {}, {}
    slot, tick = 0, 0
    while slot < len(behind) + BACK_LAG * last:
        plan = {s: ahead[tick - s] for s in range(sections) if 0 <= tick - s < len(ahead)}
        if plan:
            sizes = tuple(sorted({size for s, (_, size) in plan.items() if s < last}))
            values, state = run_forward(
                plan, limits, incoming, sizes, w_in, w_out, vecs, state
            )
            incoming = send_pages(values, plan, 1, sections)
        tick += 1
        done = sum(size for _, size in ahead[: max(tick - last, 0)])
        if slot < len(behind) and sum(behind[slot]) > done:
            continue
        plan = {
            s: behind[slot - BACK_LAG * (last - s)]
            for s in range(sections)
            if 0 <= slot - BACK_LAG * (last - s) < len(behind)
        }
        sizes = tuple(sorted({size for s, (_, size) in plan.items() if s > 0}))
        final = slot == len(behind) + BACK_LAG * last - 1
        values, state, back = run_backward(
            plan, upstream.pop(slot, {}), sizes, sections, w_in, w_out, vecs, state, back,
            phase="tail" if final else None,
        )
        upstream[slot + BACK_LAG] = send_pages(values, plan, -1, sections)
        slot += 1

    def parts(state, back):
        return (state[0], state[2], state[3], back[1]), (state[1], back[0]), back[2]

    def late(token):
        _, *both, token = run_backward(
            plan, {}, (), sections, w_in, w_out, vecs, state, back, phase="rest", token=token
        )
        return parts(*both), token

    token = jnp.zeros(TOKEN, F32)
    if dp_size == 8:
        (grad_in, grad_out), (outputs, grads), small = sum_over_line(
            token, parts(state, back)[0], late
        )
    else:
        (factors, (outputs, grads), small), token = late(token)
        small = SmallSum(small)
        so_far = ()
        for k in range(CHUNKS):
            (own, other), _, _, token = run_work(token, factors, k, None, None, ())
            pair = jnp.where(core == 0, jnp.stack([own, other]), jnp.stack([other, own]))
            pair = lax.psum(pair, "dp")
            pair = jnp.where(core == 0, pair, pair[::-1])
            _, so_far, _, token = run_work(
                token, factors, None, (pair[0], pair[1]), k, so_far
            )
        grad_in, grad_out = so_far
        while not small.done():
            token = small.advance(token)
    grad_gain, grad_bias, grad_gate = small.total
    return (
        outputs[None],
        grads[None],
        grad_in[None],
        grad_out[None],
        grad_gain,
        grad_bias,
        grad_gate[None],
    )


def solution(mesh):
    return jax.shard_map(
        body,
        mesh=mesh,
        in_specs=(
            P("dp", None),
            P("dp", None),
            P("dp", None),
            P("section", None, None),
            P("section", None, None),
            P("section", None),
            P("section", None),
            P("section", None, None),
        ),
        out_specs=(
            P("section", "dp", None),
            P("section", "dp", None),
            P("section", None, None),
            P("section", None, None),
            P("section", None),
            P("section", None),
            P("section", None, None),
        ),
        check_vma=False,
    )
```

```python
import functools

import jax
import jax.numpy as jnp
from jax import lax
from jax.experimental import pallas as pl
from jax.experimental.pallas import tpu as pltpu
from jax.sharding import PartitionSpec as P

HEAD_DIM = 64
VIS = 16
TXT = 112
PAGE = VIS + TXT
SCORE_SCALE = 0.125
MASK_FILL = -1e30
CHUNKS = 12
LAG = 3
AHEAD = 2
EARLY = 4
TOGETHER = 6
BACK_LAG = 1
FORWARD = (2, 2, 2, 2)
BACKWARD = (2, 2, 2, 2)
GELU_A = 0.7978845608028654
GELU_B = 0.044715
F32 = jnp.float32
BF16 = jnp.bfloat16

VMEM = pl.BlockSpec(memory_space=pltpu.VMEM)
SMEM = pl.BlockSpec(memory_space=pltpu.SMEM)
HBM = pl.BlockSpec(memory_space=pltpu.HBM)


def dot(a, b):
    return jnp.dot(a, b, preferred_element_type=F32)


def dot_nt(a, b):
    return lax.dot_general(a, b, (((1,), (1,)), ((), ())), preferred_element_type=F32)


def dot_tn(a, b):
    return lax.dot_general(a, b, (((0,), (0,)), ((), ())), preferred_element_type=F32)


def text_of(value):
    pages = [value[i + VIS : i + PAGE] for i in range(0, value.shape[0], PAGE)]
    return pages[0] if len(pages) == 1 else jnp.concatenate(pages, axis=0)


def visual_of(value):
    pages = [value[i : i + VIS] for i in range(0, value.shape[0], PAGE)]
    return pages[0] if len(pages) == 1 else jnp.concatenate(pages, axis=0)


def to_pages(visual, text):
    pieces = []
    for i in range(visual.shape[0] // VIS):
        pieces += [visual[i * VIS : (i + 1) * VIS], text[i * TXT : (i + 1) * TXT]]
    return jnp.concatenate(pieces, axis=0)


def gate_table(vecs, rows, width):
    visual = lax.broadcasted_iota(jnp.int32, (rows, width), 0) % PAGE < VIS
    return jnp.where(visual, vecs[3:4, :], vecs[2:3, :])


def tail_parts(x, branch, gate_rows):
    gate = jax.nn.sigmoid(jnp.sum(x * gate_rows, axis=-1, keepdims=True))
    mixed = x + gate * branch
    centred = mixed - jnp.mean(mixed, axis=-1, keepdims=True)
    inv = lax.rsqrt(jnp.mean(centred * centred, axis=-1, keepdims=True) + 1e-05)
    return gate, centred * inv, inv


def allowed_pairs(limit_row, cross):
    key = lax.broadcasted_iota(jnp.int32, (PAGE, 2 * PAGE), 0)
    query = lax.broadcasted_iota(jnp.int32, (PAGE, 2 * PAGE), 1) % PAGE
    limit = jnp.where(key < VIS, limit_row[:, : 2 * PAGE], limit_row[:, 2 * PAGE :])
    unlike = jnp.where(query < VIS, 1, 0) + jnp.where(key < VIS, 1, 0) - 1
    return key + (PAGE * cross) * (unlike * unlike) < limit


def low_lanes(shape):
    return lax.broadcasted_iota(jnp.int32, shape, 1) < HEAD_DIM


def stack_heads(pair):
    low = low_lanes(pair.shape)
    zero = jnp.zeros_like(pair)
    return jnp.concatenate([jnp.where(low, pair, zero), jnp.where(low, zero, pair)], axis=0)


def unstack_heads(stacked):
    half = stacked.shape[0] // 2
    top = stacked[:half]
    return jnp.where(low_lanes(top.shape), top, stacked[half:])


def masked_softmax(scores, allowed):
    scores = jnp.where(allowed, scores * SCORE_SCALE, MASK_FILL)
    weights = jnp.exp(scores - jnp.max(scores, axis=0, keepdims=True))
    return weights / jnp.sum(weights, axis=0, keepdims=True)


def load_kernel(*refs, count):
    sources, live_in = refs[: count + 3], refs[count + 3]
    vecs, limits = refs[count + 4 : count + 6]
    targets = refs[count + 6 : 2 * count + 6]
    gain, bias, gates, live, sems = refs[2 * count + 6 :]
    targets = (*targets, gain, bias, gates)
    copies = [
        pltpu.make_async_copy(source, target, sems.at[i])
        for i, (source, target) in enumerate(zip(sources, targets))
    ]
    live_copy = pltpu.make_async_copy(live_in, live, sems.at[count + 3])
    for copy in copies[count:] + [live_copy] + copies[:count]:
        copy.start()
    for copy in copies[count:] + [live_copy]:
        copy.wait()
    vecs[0:1, :] = gain[...]
    vecs[1:2, :] = bias[...]
    vecs[2:4, :] = gates[...]
    first = lax.broadcasted_iota(jnp.int32, (1, 4 * PAGE), 1) < 2 * PAGE
    for page in range(limits.shape[0]):
        limits[page : page + 1, :] = jnp.where(first, live[0, page], live[1, page] + VIS)
    for copy in copies[:count]:
        copy.wait()


def block(index, size):
    if isinstance(index, int):
        return slice(index * size, (index + 1) * size)
    return pl.ds(pl.multiple_of(index * size, size), size)


def page_rows(first_page, i):
    return pl.ds(pl.multiple_of((first_page + i) * PAGE, PAGE), PAGE)


def each_group(plan, section, run):
    groups = {}
    for s, (page, size) in plan.items():
        groups.setdefault((s % 2, size), []).append((s, page))
    for (odd, size), members in groups.items():
        here, first = section == members[0][0], members[0][1]
        for s, page in members[1:]:
            here = jnp.logical_or(here, section == s)
            first = jnp.where(section == s, page, first)

        @pl.when(here)
        def _():
            run(odd == 0, first, size * PAGE)


def forward_kernel(limits, w_in, w_out, vecs, *refs, state_in, plan, sizes_in, sizes_out):
    incoming = dict(zip(sizes_in, refs))
    refs = refs[len(sizes_in) + state_in :]
    outgoing = dict(zip(sizes_out, refs))
    state = refs[len(sizes_out) :]
    section = lax.axis_index("section")

    def run(is_attention, page, micro):
        size = micro // PAGE
        part = (limits, incoming.get(size), w_in, w_out, vecs, outgoing.get(size), *state)
        forward_part(*part, section, page, micro, is_attention)

    each_group(plan, section, run)


def forward_part(
    limits, incoming, w_in, w_out, vecs, y_ref, xin, out, sav, dh, br, probs_ref,
    section, page, micro, is_attention,
):
    width = xin.shape[1]
    group = micro // PAGE
    cross = jnp.where(section == 0, 1, 0)
    rows = pl.ds(pl.multiple_of(page * PAGE, PAGE), micro)

    def begin():
        x_low = xin[rows, :]
        if incoming is not None:
            x_low = jnp.where(section == 0, x_low, incoming[...])
        xin[rows, :] = x_low
        return x_low

    def finish(x_low, branch):
        br[rows, :] = branch
        gate, normed, inv = tail_parts(
            x_low.astype(F32), branch, gate_table(vecs, micro, width)
        )
        y = (normed * vecs[0:1, :] + vecs[1:2, :]).astype(BF16)
        if y_ref is not None:
            y_ref[...] = y
        out[rows, :] = y

    def attention():
        x_low = begin()
        x_text, x_visual = text_of(x_low), visual_of(x_low)

        for k in range(3):
            cols = block(k, width)
            sav[rows, cols] = to_pages(
                dot(x_visual, w_out[cols, :]).astype(BF16), dot(x_text, w_in[:, cols]).astype(BF16)
            )

        for i in range(group):
            here = page_rows(page, i)
            allowed = allowed_pairs(limits[pl.ds(page + i, 1), :], cross)
            pairs = width // (2 * HEAD_DIM)

            for first in range(0, pairs, TOGETHER):
                some = range(first, first + TOGETHER)
                scores = [
                    dot_nt(
                        sav[here, block(pairs + n, 128)],
                        stack_heads(sav[here, block(n, 128)]),
                    )
                    for n in some
                ]
                probs = [masked_softmax(one, allowed).astype(BF16) for one in scores]
                contexts = [
                    dot_tn(one, sav[here, block(2 * pairs + n, 128)])
                    for n, one in zip(some, probs)
                ]
                for n, one, context in zip(some, probs, contexts):
                    probs_ref[here, block(n, 2 * PAGE)] = one
                    sav[here, block(3 * pairs + n, 128)] = unstack_heads(context).astype(BF16)

        context = sav[rows, 3 * width :]
        finish(
            x_low,
            to_pages(
                dot(visual_of(context), w_out[3 * width :, :]),
                dot(text_of(context), w_in[:, 3 * width :]),
            ),
        )

    def feed():
        x_low = begin()

        hidden_width = w_in.shape[1]
        branch = None
        ahead = dot(x_low, w_in[:, :width])
        for start in range(0, hidden_width, width):
            cols = slice(start, start + width)
            hidden = ahead
            if start + width < hidden_width:
                ahead = dot(x_low, w_in[:, start + width : start + 2 * width])
            square = hidden * hidden
            tanh = jnp.tanh(hidden * (GELU_A + (GELU_A * GELU_B) * square))
            half = 0.5 + 0.5 * tanh
            active = hidden * half
            low = active.astype(BF16)
            sav[rows, cols] = low
            slope = half + (active * (1.0 - tanh)) * (
                GELU_A + (3.0 * GELU_A * GELU_B) * square
            )
            dh[rows, cols] = slope.astype(BF16)
            part = dot(low, w_out[cols, :])
            branch = part if branch is None else branch + part
        finish(x_low, branch)

    (attention if is_attention else feed)()


def backward_kernel(
    w_in, w_out, vecs, *refs, state_in, plan, sizes_in, sizes_out, sections, phase
):
    incoming = dict(zip(sizes_in, refs))
    late = phase == "rest"
    refs = refs[len(sizes_in) + late + state_in :]
    outgoing = dict(zip(sizes_out, refs))
    state, dc = refs[len(sizes_out) : -1 - late], refs[-1]
    if late:
        refs[-2][...] = jnp.zeros_like(refs[-2])
    section = lax.axis_index("section")

    def run(is_attention, page, micro):
        size = micro // PAGE
        part = (incoming.get(size), w_in, w_out, vecs, outgoing.get(size), *state, dc)
        backward_part(*part, section == sections - 1, page, micro, is_attention, phase)

    each_group(plan, section, run)


def backward_part(
    incoming, w_in, w_out, vecs, dx_ref, xin, out, sav, dh, br, probs_ref, grads, db, small, dc,
    is_last, page, micro, is_attention, phase,
):
    width = xin.shape[1]
    group = micro // PAGE
    rows = pl.ds(pl.multiple_of(page * PAGE, PAGE), micro)

    def tail():
        x = xin[rows, :].astype(F32)
        branch = br[rows, :]
        gate_rows = gate_table(vecs, micro, width)
        gate, normed, inv = tail_parts(x, branch, gate_rows)
        dy = grads[rows, :]
        if incoming is not None:
            dy = jnp.where(is_last, dy, incoming[...])
        dy = dy.astype(F32)
        dn = dy * vecs[0:1, :]
        du = inv * (
            dn
            - jnp.mean(dn, axis=-1, keepdims=True)
            - normed * jnp.mean(dn * normed, axis=-1, keepdims=True)
        )
        dbranch = (du * gate).astype(BF16)
        db[rows, :] = dbranch
        dz = jnp.sum(du * branch, axis=-1, keepdims=True) * gate * (1.0 - gate)
        weighted = dz * x
        sums = jnp.concatenate(
            [
                jnp.sum(dy * normed, axis=0, keepdims=True),
                jnp.sum(dy, axis=0, keepdims=True),
                jnp.sum(text_of(weighted), axis=0, keepdims=True),
                jnp.sum(visual_of(weighted), axis=0, keepdims=True),
                jnp.zeros((4, width), F32),
            ],
            axis=0,
        )
        small[pl.ds(pl.multiple_of(page * 8, 8), 8), :] = sums
        for i in range(1, group):
            small[pl.ds(pl.multiple_of((page + i) * 8, 8), 8), :] = jnp.zeros_like(sums)
        br[rows, :] = du + dz * gate_rows

    def finish(total):
        dx = total.astype(BF16)
        if dx_ref is not None:
            dx_ref[...] = dx
        grads[rows, :] = dx

    def attention():
        if phase != "rest":
            tail()
        if phase == "tail":
            return
        dbranch = db[rows, :]
        dc[:micro, :] = to_pages(
            dot_nt(visual_of(dbranch), w_out[3 * width :, :]).astype(BF16),
            dot_nt(text_of(dbranch), w_in[:, 3 * width :]).astype(BF16),
        )
        for i in range(group):
            here = page_rows(page, i)
            own = slice(i * PAGE, (i + 1) * PAGE)
            pairs = width // (2 * HEAD_DIM)

            for first in range(0, pairs, TOGETHER):
                some = range(first, first + TOGETHER)
                contexts = [stack_heads(dc[own, block(n, 128)]) for n in some]
                dprobs = [
                    dot_nt(sav[here, block(2 * pairs + n, 128)], one)
                    for n, one in zip(some, contexts)
                ]
                low = [probs_ref[here, block(n, 2 * PAGE)] for n in some]
                dvalues = [dot(one, context) for one, context in zip(low, contexts)]
                dscores = []
                for one, change in zip(low, dprobs):
                    probs = one.astype(F32)
                    mean = jnp.sum(change * probs, axis=0, keepdims=True)
                    dscores.append((probs * (change - mean)).astype(BF16))
                dkeys = [
                    dot(one, stack_heads(sav[here, block(n, 128)]))
                    for n, one in zip(some, dscores)
                ]
                dqueries = [
                    dot_tn(one, sav[here, block(pairs + n, 128)])
                    for n, one in zip(some, dscores)
                ]
                for n, dquery, dkey, dvalue in zip(some, dqueries, dkeys, dvalues):
                    dh[here, block(2 * pairs + n, 128)] = dvalue.astype(BF16)
                    dh[here, block(pairs + n, 128)] = (dkey * SCORE_SCALE).astype(BF16)
                    dh[here, block(n, 128)] = (unstack_heads(dquery) * SCORE_SCALE).astype(BF16)

        text, visual = None, None
        for k in range(3):
            cols = slice(k * width, (k + 1) * width)
            part = dh[rows, cols]
            one = dot_nt(text_of(part), w_in[:, cols])
            two = dot_nt(visual_of(part), w_out[cols, :])
            text = one if text is None else text + one
            visual = two if visual is None else visual + two
        finish(br[rows, :] + to_pages(visual, text))

    def feed():
        if phase != "rest":
            tail()
        if phase == "tail":
            return
        dbranch, total = db[rows, :], br[rows, :]
        for start in range(0, w_in.shape[1], width):
            cols = slice(start, start + width)
            dhidden = (dot_nt(dbranch, w_out[cols, :]) * dh[rows, cols].astype(F32)).astype(BF16)
            dh[rows, cols] = dhidden
            total = total + dot_nt(dhidden, w_in[:, cols])
        finish(total)

    (attention if is_attention else feed)()


def weight_chunk(kind, core, xin, sav, dh, db, own_ref, other_ref, chunk):
    part, width = own_ref.shape
    start = chunk * part
    cols = slice(start, start + part)

    def put(grad_a, grad_b):
        low_a = jnp.concatenate(
            [grad_a[i : i + part].astype(BF16) for i in range(0, width, part)], axis=1
        )
        low_b = grad_b.astype(BF16)
        own_ref[...] = jnp.where(core == 0, low_a, low_b)
        other_ref[...] = jnp.where(core == 0, low_b, low_a)

    @pl.when(kind == 1)
    def attention():
        block, inner = start // width, start % width
        inner_cols = slice(inner, inner + part)
        if block < 3:
            left, right = xin[...], dh[:, block * width : (block + 1) * width]
            put(
                dot_tn(text_of(left), text_of(dh[:, cols])),
                dot_tn(visual_of(left[:, inner_cols]), visual_of(right)),
            )
        else:
            left, right = sav[:, 3 * width :], db[...]
            put(
                dot_tn(text_of(left), text_of(right[:, inner_cols])),
                dot_tn(visual_of(left[:, inner_cols]), visual_of(right)),
            )

    @pl.when(kind == 2)
    def feed():
        put(dot_tn(xin[...], dh[:, cols]), dot_tn(sav[:, cols], db[...]))


def work_kernel(*refs, chunk, place, placed, flush):
    refs = list(refs)
    del refs[0]
    core = lax.axis_index("dp") % 2

    def take(count):
        taken = refs[:count]
        del refs[:count]
        return taken

    factors = take(4) if chunk is not None else None
    rows_in = take(flush)
    if place is not None:
        own, other = take(2)
        take(placed)
    partial = take(2) if chunk is not None else None
    rows_out = take(flush)
    if place is not None:
        grad_in, grad_out = take(2)
    (token,) = take(1)
    token[...] = jnp.zeros_like(token)
    copies = []
    if flush:
        row_sems = refs.pop()
        for i, (source, target) in enumerate(zip(rows_in, rows_out)):
            copies.append(pltpu.make_async_copy(source, target, row_sems.at[i]))
            copies[-1].start()
    if place is not None:
        buf_a, buf_b, sems = refs
        part, width = buf_b.shape
        start = place * part
        mine, theirs = own[...], other[...]
        buf_b[...] = jnp.where(core == 0, theirs, mine).astype(F32)
        copies.append(
            pltpu.make_async_copy(buf_b, grad_out.at[pl.ds(start, part), :], sems.at[0])
        )
        copies[-1].start()
        for i in range(width // part):
            cols = slice(i * part, (i + 1) * part)
            buf_a[cols, :] = jnp.where(core == 0, mine[:, cols], theirs[:, cols]).astype(F32)
        copies.append(
            pltpu.make_async_copy(buf_a, grad_in.at[:, pl.ds(start, part)], sems.at[1])
        )
        copies[-1].start()
    if chunk is not None:
        kind = 1 + lax.axis_index("section") % 2
        weight_chunk(kind, core, *factors, *partial, chunk)
    for copy in copies:
        copy.wait()


def add_low(a, b):
    return (a.astype(F32) + b.astype(F32)).astype(BF16)


def outer_kernel(*refs, new, total):
    refs = list(refs)
    del refs[0]
    chip = lax.axis_index("dp") // 2
    new_in = [refs.pop(0)[...] for _ in range(2 * new)]
    total_in = [refs.pop(0)[...] for _ in range(2 * total)]
    values = []
    if new:
        values.append(add_low(*new_in))
        refs.pop(0)[...] = values[-1]
    if total:
        values.append(add_low(*total_in))
        refs.pop(0)[...] = values[-1]
    if new and total:
        middle = jnp.logical_or(chip == 1, chip == 2)
        refs.pop(0)[...] = jnp.where(middle, values[1], values[0])
    token = refs.pop(0)
    token[...] = jnp.zeros_like(token)


def inner_kernel(*refs, inner, final):
    refs = list(refs)
    del refs[0]
    chip = lax.axis_index("dp") // 2
    got = refs.pop(0)[...]
    first = refs.pop(0)[...] if inner else None
    total = refs.pop(0)[...] if final else None
    if inner:
        refs.pop(0)[...] = add_low(first, got)
    if final:
        middle = jnp.logical_or(chip == 1, chip == 2)
        refs.pop(0)[...] = jnp.where(middle, total, got)
    token = refs.pop(0)
    token[...] = jnp.zeros_like(token)


def sum_pages_kernel(token_in, small, total_ref, token):
    total = small[0:8, :]
    for i in range(8, small.shape[0], 8):
        total += small[i : i + 8, :]
    total_ref[...] = total
    token[...] = jnp.zeros_like(token)


def add_kernel(token_in, a, b, *refs):
    total = a[...] + b[...]
    *outs, token = refs
    token[...] = jnp.zeros_like(token)
    if len(outs) == 1:
        outs[0][...] = total
    else:
        gain, bias, gates = outs
        gain[...] = total[0:1]
        bias[...] = total[1:2]
        gates[...] = total[2:4]


def struct(shape, dtype):
    return jax.ShapeDtypeStruct(shape, dtype)


def params(mebibytes):
    return pltpu.CompilerParams(vmem_limit_bytes=mebibytes << 20)


def in_vmem(*arrays):
    return [pltpu.with_memory_space_constraint(a, pltpu.VMEM) for a in arrays]


def run_load(gain, bias, gates, counts, *arrays):
    width = gain.shape[1]
    inputs = [*arrays, gain, bias, gates, counts.T]
    return pl.pallas_call(
        functools.partial(load_kernel, count=len(arrays)),
        out_shape=[struct((8, width), F32), struct((counts.shape[0], 4 * PAGE), jnp.int32)]
        + [pltpu.VMEM(a.shape, a.dtype) for a in arrays],
        in_specs=[HBM] * len(inputs),
        out_specs=[VMEM] * (2 + len(arrays)),
        scratch_shapes=[
            pltpu.VMEM((1, width), F32),
            pltpu.VMEM((1, width), F32),
            pltpu.VMEM((2, width), F32),
            pltpu.SMEM((2, counts.shape[0]), jnp.int32),
            pltpu.SemaphoreType.DMA((len(inputs),)),
        ],
        compiler_params=params(4),
        name="load_weights",
    )(*[pltpu.with_memory_space_constraint(a, pltpu.HBM) for a in inputs])


def run_forward(plan, limits, incoming, sizes_out, w_in, w_out, vecs, state):
    rows, width = state[0].shape
    hidden = w_in.shape[1]
    sizes_in = tuple(incoming)
    first = 4 + len(sizes_in)
    got = pl.pallas_call(
        functools.partial(
            forward_kernel,
            state_in=len(state), plan=plan, sizes_in=sizes_in, sizes_out=sizes_out,
        ),
        out_shape=[struct((size * PAGE, width), BF16) for size in sizes_out]
        + [
            pltpu.VMEM((rows, width), BF16),
            pltpu.VMEM((rows, width), BF16),
            pltpu.VMEM((rows, hidden), BF16),
            pltpu.VMEM((rows, hidden), BF16),
            pltpu.VMEM((rows, width), F32),
            pltpu.VMEM((rows, 2 * PAGE * (width // (2 * HEAD_DIM))), BF16),
        ],
        in_specs=[VMEM] * (first + len(state)),
        out_specs=[VMEM] * (len(sizes_out) + 6),
        input_output_aliases={first + i: len(sizes_out) + i for i in range(len(state))},
        compiler_params=params(12),
        name="forward_pages",
    )(limits, *in_vmem(w_in, w_out), vecs, *incoming.values(), *state)
    return dict(zip(sizes_out, got)), got[len(sizes_out) :]


def run_backward(
    plan, incoming, sizes_out, sections, w_in, w_out, vecs, state, back, phase=None, token=None
):
    rows, width = back[0].shape
    every = list(state) + list(back)
    sizes_in = tuple(incoming)
    late = [] if token is None else [token]
    first = 3 + len(sizes_in) + len(late)
    largest = max(size for _, size in plan.values())
    got = pl.pallas_call(
        functools.partial(
            backward_kernel,
            state_in=len(every), plan=plan, sizes_in=sizes_in, sizes_out=sizes_out,
            sections=sections, phase=phase,
        ),
        out_shape=[struct((size * PAGE, width), BF16) for size in sizes_out]
        + [pltpu.VMEM(s.shape, s.dtype) for s in state]
        + [
            pltpu.VMEM((rows, width), BF16),
            pltpu.VMEM((rows, width), BF16),
            pltpu.VMEM((8 * rows // PAGE, width), F32),
        ]
        + [struct(TOKEN, F32) for _ in late],
        in_specs=[VMEM] * (first + len(every)),
        out_specs=[VMEM] * (len(sizes_out) + 9 + len(late)),
        input_output_aliases={first + i: len(sizes_out) + i for i in range(len(every))},
        scratch_shapes=[pltpu.VMEM((largest * PAGE, width), BF16)],
        compiler_params=params(12),
        name="backward_pages",
    )(*in_vmem(w_in, w_out), vecs, *incoming.values(), *late, *every)
    state_out = got[len(sizes_out) :]
    return dict(zip(sizes_out, got)), state_out[:6], state_out[6:9], *state_out[9:]


def send_pages(values, plan, step, sections):
    sent = {}
    for size, value in values.items():
        pairs = [
            (s, s + step)
            for s, (_, own) in plan.items()
            if own == size and 0 <= s + step < sections
        ]
        sent[size] = lax.ppermute(value, "section", pairs)
    return sent


def micro_batches(sizes, pages):
    if sum(sizes) != pages:
        sizes = (1,) * pages
    starts = [sum(sizes[:i]) for i in range(len(sizes))]
    return list(zip(starts, sizes))


TOKEN = (8, 128)


def run_work(token, factors, chunk, totals, place, grads, flush=()):
    width = factors[0].shape[1]
    hidden = factors[1].shape[1]
    part = hidden // CHUNKS
    inputs, specs = [token], [VMEM]
    outs, out_specs, scratch, aliases = [], [], [], {}
    if chunk is not None:
        inputs += in_vmem(*factors)
        specs += [VMEM] * 4
        outs += [struct((part, width), BF16)] * 2
        out_specs += [VMEM] * 2
    if flush:
        inputs += in_vmem(*flush)
        specs += [VMEM] * len(flush)
        outs += [pltpu.HBM(a.shape, a.dtype) for a in flush]
        out_specs += [HBM] * len(flush)
    if place is not None:
        inputs += list(totals)
        specs += [VMEM] * 2
        aliases = {len(inputs) + i: len(outs) + i for i in range(len(grads))}
        inputs += list(grads)
        specs += [HBM] * len(grads)
        outs += [pltpu.HBM((width, hidden), F32), pltpu.HBM((hidden, width), F32)]
        out_specs += [HBM] * 2
        scratch = [
            pltpu.VMEM((width, part), F32),
            pltpu.VMEM((part, width), F32),
            pltpu.SemaphoreType.DMA((2,)),
        ]
    if flush:
        scratch.append(pltpu.SemaphoreType.DMA((len(flush),)))
    *got, token = pl.pallas_call(
        functools.partial(
            work_kernel, chunk=chunk, place=place, placed=len(grads), flush=len(flush)
        ),
        out_shape=outs + [struct(TOKEN, F32)],
        in_specs=specs,
        out_specs=out_specs + [VMEM],
        input_output_aliases=aliases,
        scratch_shapes=scratch,
        compiler_params=params(16),
        name="work_beside",
    )(*inputs)
    made = [got.pop(0) for _ in range(2)] if chunk is not None else None
    flushed = [got.pop(0) for _ in flush]
    return made, (got if place is not None else grads), flushed, token


def run_step(kernel, name, inputs, outs):
    return pl.pallas_call(
        kernel,
        out_shape=[struct(inputs[-1].shape, inputs[-1].dtype)] * outs + [struct(TOKEN, F32)],
        in_specs=[VMEM] * len(inputs),
        out_specs=[VMEM] * (outs + 1),
        compiler_params=params(8),
        name=name,
    )(*inputs)


class SmallSum:
    def __init__(self, small):
        self.small = small
        self.size = lax.axis_size("dp")
        self.step = 0
        self.total = None
        self.got = None

    def advance(self, token):
        if self.step == 0:
            self.total, token = pl.pallas_call(
                sum_pages_kernel,
                out_shape=[struct((8, self.small.shape[1]), F32), struct(TOKEN, F32)],
                in_specs=[VMEM, VMEM],
                out_specs=[VMEM, VMEM],
                compiler_params=params(4),
                name="small_sum",
            )(token, *in_vmem(self.small))
            self.step = 1
        elif self.got is not None:
            width = self.total.shape[1]
            heights = (8,) if self.step < self.size else (1, 1, 2)
            *outs, token = pl.pallas_call(
                add_kernel,
                out_shape=[struct((h, width), F32) for h in heights] + [struct(TOKEN, F32)],
                in_specs=[VMEM] * 3,
                out_specs=[VMEM] * (len(heights) + 1),
                compiler_params=params(4),
                name="small_sum",
            )(token, self.total, self.got)
            self.total = outs[0] if len(heights) == 1 else outs
            self.got = None
        if self.step < self.size:
            pairs = [(i, i ^ self.step) for i in range(self.size)]
            self.got = lax.ppermute(self.total, "dp", pairs)
            self.step *= 2
        return token

    def done(self):
        return self.step >= self.size and self.got is None


def sum_over_line(token, factors, late):
    count = CHUNKS
    order = [(k + count * 3 // 4) % count for k in range(count)]
    small, flush = None, ()
    swap = [(i, i ^ 1) for i in range(8)]
    outer = [(i, i ^ 2) for i in range(8)]
    middle = [(2, 4), (3, 5), (4, 2), (5, 3)]
    lag = LAG
    made, firsts, inners, totals, finals = {}, {}, {}, {}, {}
    got_outer, got_inner = {}, {}
    grads, flushed = (), None

    def work(token, grads, chunk, place, flush=()):
        chunk = chunk if chunk is not None and chunk < count else None
        place = place if place is not None and 0 <= place < count else None
        if chunk is None and place is None:
            return token, grads, ()
        pair = finals.pop(place) if place is not None else None
        new, grads, flushed, token = run_work(
            token,
            factors,
            None if chunk is None else order[chunk],
            pair,
            None if place is None else order[place],
            grads,
            flush,
        )
        if new:
            made[chunk] = (new[0], lax.ppermute(new[1], "dp", swap))
        return token, grads, flushed

    for k in range(AHEAD):
        token, grads, _ = work(token, grads, k, None)

    def at(half, stage):
        k, odd = divmod(half - stage * lag, 2)
        return k if not odd and 0 <= k < count else None

    for half in range(2 * count - 1 + 3 * lag):
        if half % 2 == 0:
            new, total = at(half, 0), at(half, 2)
            inputs = [token]
            if new is not None:
                inputs += made.pop(new)
            if total is not None:
                inputs += [inners.pop(total), got_inner.pop(half - lag)]
            if len(inputs) > 1:
                both = new is not None and total is not None
                kernel = functools.partial(
                    outer_kernel, new=int(new is not None), total=int(total is not None)
                )
                *outs, token = run_step(kernel, "outer_step", inputs, 2 + 1 if both else 1)
                send = outs[-1]
                if new is not None:
                    firsts[new] = outs[0]
                if total is not None:
                    totals[total] = outs[1 if both else 0]
                got_outer[half] = lax.ppermute(send, "dp", outer)
            if half == 2:
                (factors, flush, rows), token = late(token)
                small = SmallSum(rows)
                for k in range(AHEAD + 1, AHEAD + 1 + EARLY):
                    token, grads, rows = work(token, grads, k, None, flush)
                    flush, flushed = (), rows or flushed
            if half >= 4 and half % 4 == 0 and not small.done():
                token = small.advance(token)
        else:
            inner, final = at(half, 1), at(half, 3)
            if inner is not None or final is not None:
                inputs = [token, got_outer.pop(half - lag)]
                if inner is not None:
                    inputs.append(firsts.pop(inner))
                if final is not None:
                    inputs.append(totals.pop(final))
                kernel = functools.partial(
                    inner_kernel, inner=inner is not None, final=final is not None
                )
                *outs, token = run_step(
                    kernel, "inner_step", inputs, (inner is not None) + (final is not None)
                )
                if inner is not None:
                    inners[inner] = outs[0]
                    got_inner[half] = lax.ppermute(outs[0], "dp", middle)
                if final is not None:
                    finals[final] = (outs[-1], lax.ppermute(outs[-1], "dp", swap))
            chunk = (half - 1) // 2 + AHEAD + (EARLY if half > 1 else 0)
            token, grads, _ = work(token, grads, chunk, at(half - 2, 3))
    token, grads, _ = work(token, grads, None, count - 1)
    while not small.done():
        token = small.advance(token)
    return grads, flushed, small


def body(acts, cotan, counts, weight_in, weight_out, ln_gain, ln_bias, gate_vec):
    sections = lax.axis_size("section")
    dp_index = lax.axis_index("dp")
    dp_size = lax.axis_size("dp")
    rows, width = acts.shape
    vecs, limits, w_in, w_out, acts, cotan = run_load(
        ln_gain, ln_bias, gate_vec[0], counts, weight_in[0], weight_out[0], acts, cotan
    )
    core = dp_index % 2
    ahead = micro_batches(FORWARD, rows // PAGE)
    behind = micro_batches(BACKWARD, rows // PAGE)
    last = sections - 1
    state, back = (acts,), (cotan,)
    incoming, upstream = {}, {}
    slot, tick = 0, 0
    while slot < len(behind) + BACK_LAG * last:
        plan = {s: ahead[tick - s] for s in range(sections) if 0 <= tick - s < len(ahead)}
        if plan:
            sizes = tuple(sorted({size for s, (_, size) in plan.items() if s < last}))
            values, state = run_forward(
                plan, limits, incoming, sizes, w_in, w_out, vecs, state
            )
            incoming = send_pages(values, plan, 1, sections)
        tick += 1
        done = sum(size for _, size in ahead[: max(tick - last, 0)])
        if slot < len(behind) and sum(behind[slot]) > done:
            continue
        plan = {
            s: behind[slot - BACK_LAG * (last - s)]
            for s in range(sections)
            if 0 <= slot - BACK_LAG * (last - s) < len(behind)
        }
        sizes = tuple(sorted({size for s, (_, size) in plan.items() if s > 0}))
        final = slot == len(behind) + BACK_LAG * last - 1
        values, state, back = run_backward(
            plan, upstream.pop(slot, {}), sizes, sections, w_in, w_out, vecs, state, back,
            phase="tail" if final else None,
        )
        upstream[slot + BACK_LAG] = send_pages(values, plan, -1, sections)
        slot += 1

    def parts(state, back):
        return (state[0], state[2], state[3], back[1]), (state[1], back[0]), back[2]

    def late(token):
        _, *both, token = run_backward(
            plan, {}, (), sections, w_in, w_out, vecs, state, back, phase="rest", token=token
        )
        return parts(*both), token

    token = jnp.zeros(TOKEN, F32)
    if dp_size == 8:
        (grad_in, grad_out), (outputs, grads), small = sum_over_line(
            token, parts(state, back)[0], late
        )
    else:
        (factors, (outputs, grads), small), token = late(token)
        small = SmallSum(small)
        so_far = ()
        for k in range(CHUNKS):
            (own, other), _, _, token = run_work(token, factors, k, None, None, ())
            pair = jnp.where(core == 0, jnp.stack([own, other]), jnp.stack([other, own]))
            pair = lax.psum(pair, "dp")
            pair = jnp.where(core == 0, pair, pair[::-1])
            _, so_far, _, token = run_work(
                token, factors, None, (pair[0], pair[1]), k, so_far
            )
        grad_in, grad_out = so_far
        while not small.done():
            token = small.advance(token)
    grad_gain, grad_bias, grad_gate = small.total
    return (
        outputs[None],
        grads[None],
        grad_in[None],
        grad_out[None],
        grad_gain,
        grad_bias,
        grad_gate[None],
    )


def solution(mesh):
    return jax.shard_map(
        body,
        mesh=mesh,
        in_specs=(
            P("dp", None),
            P("dp", None),
            P("dp", None),
            P("section", None, None),
            P("section", None, None),
            P("section", None),
            P("section", None),
            P("section", None, None),
        ),
        out_specs=(
            P("section", "dp", None),
            P("section", "dp", None),
            P("section", None, None),
            P("section", None, None),
            P("section", None),
            P("section", None),
            P("section", None, None),
        ),
        check_vma=False,
    )
```

```python
import functools

import jax
import jax.numpy as jnp
from jax import lax
from jax.experimental import pallas as pl
from jax.experimental.pallas import tpu as pltpu
from jax.sharding import PartitionSpec as P

HEAD_DIM = 64
VIS = 16
TXT = 112
PAGE = VIS + TXT
SCORE_SCALE = 0.125
MASK_FILL = -1e30
CHUNKS = 12
LAG = 3
AHEAD = 2
EARLY = 4
TOGETHER = 6
BACK_LAG = 1
FORWARD = (2, 2, 2, 2)
BACKWARD = (2, 2, 2, 2)
GELU_A = 0.7978845608028654
GELU_B = 0.044715
F32 = jnp.float32
BF16 = jnp.bfloat16

VMEM = pl.BlockSpec(memory_space=pltpu.VMEM)
SMEM = pl.BlockSpec(memory_space=pltpu.SMEM)
HBM = pl.BlockSpec(memory_space=pltpu.HBM)


def dot(a, b):
    return jnp.dot(a, b, preferred_element_type=F32)


def dot_nt(a, b):
    return lax.dot_general(a, b, (((1,), (1,)), ((), ())), preferred_element_type=F32)


def dot_tn(a, b):
    return lax.dot_general(a, b, (((0,), (0,)), ((), ())), preferred_element_type=F32)


def text_of(value):
    pages = [value[i + VIS : i + PAGE] for i in range(0, value.shape[0], PAGE)]
    return pages[0] if len(pages) == 1 else jnp.concatenate(pages, axis=0)


def visual_of(value):
    pages = [value[i : i + VIS] for i in range(0, value.shape[0], PAGE)]
    return pages[0] if len(pages) == 1 else jnp.concatenate(pages, axis=0)


def to_pages(visual, text):
    pieces = []
    for i in range(visual.shape[0] // VIS):
        pieces += [visual[i * VIS : (i + 1) * VIS], text[i * TXT : (i + 1) * TXT]]
    return jnp.concatenate(pieces, axis=0)


def gate_table(vecs, rows, width):
    visual = lax.broadcasted_iota(jnp.int32, (rows, width), 0) % PAGE < VIS
    return jnp.where(visual, vecs[3:4, :], vecs[2:3, :])


def tail_parts(x, branch, gate_rows):
    gate = jax.nn.sigmoid(jnp.sum(x * gate_rows, axis=-1, keepdims=True))
    mixed = x + gate * branch
    centred = mixed - jnp.mean(mixed, axis=-1, keepdims=True)
    inv = lax.rsqrt(jnp.mean(centred * centred, axis=-1, keepdims=True) + 1e-05)
    return gate, centred * inv, inv


def allowed_pairs(limit_row, cross):
    key = lax.broadcasted_iota(jnp.int32, (PAGE, 2 * PAGE), 0)
    query = lax.broadcasted_iota(jnp.int32, (PAGE, 2 * PAGE), 1) % PAGE
    limit = jnp.where(key < VIS, limit_row[:, : 2 * PAGE], limit_row[:, 2 * PAGE :])
    unlike = jnp.where(query < VIS, 1, 0) + jnp.where(key < VIS, 1, 0) - 1
    return key + (PAGE * cross) * (unlike * unlike) < limit


def low_lanes(shape):
    return lax.broadcasted_iota(jnp.int32, shape, 1) < HEAD_DIM


def stack_heads(pair):
    low = low_lanes(pair.shape)
    zero = jnp.zeros_like(pair)
    return jnp.concatenate([jnp.where(low, pair, zero), jnp.where(low, zero, pair)], axis=0)


def unstack_heads(stacked):
    half = stacked.shape[0] // 2
    top = stacked[:half]
    return jnp.where(low_lanes(top.shape), top, stacked[half:])


def masked_softmax(scores, allowed):
    scores = jnp.where(allowed, scores * SCORE_SCALE, MASK_FILL)
    weights = jnp.exp(scores - jnp.max(scores, axis=0, keepdims=True))
    return weights / jnp.sum(weights, axis=0, keepdims=True)


def load_kernel(*refs, count):
    sources, live_in = refs[: count + 3], refs[count + 3]
    vecs, limits = refs[count + 4 : count + 6]
    targets = refs[count + 6 : 2 * count + 6]
    gain, bias, gates, live, sems = refs[2 * count + 6 :]
    targets = (*targets, gain, bias, gates)
    copies = [
        pltpu.make_async_copy(source, target, sems.at[i])
        for i, (source, target) in enumerate(zip(sources, targets))
    ]
    live_copy = pltpu.make_async_copy(live_in, live, sems.at[count + 3])
    for copy in copies[count:] + [live_copy] + copies[:count]:
        copy.start()
    for copy in copies[count:] + [live_copy]:
        copy.wait()
    vecs[0:1, :] = gain[...]
    vecs[1:2, :] = bias[...]
    vecs[2:4, :] = gates[...]
    first = lax.broadcasted_iota(jnp.int32, (1, 4 * PAGE), 1) < 2 * PAGE
    for page in range(limits.shape[0]):
        limits[page : page + 1, :] = jnp.where(first, live[0, page], live[1, page] + VIS)
    for copy in copies[:count]:
        copy.wait()


def block(index, size):
    if isinstance(index, int):
        return slice(index * size, (index + 1) * size)
    return pl.ds(pl.multiple_of(index * size, size), size)


def page_rows(first_page, i):
    return pl.ds(pl.multiple_of((first_page + i) * PAGE, PAGE), PAGE)


def each_group(plan, section, run):
    groups = {}
    for s, (page, size) in plan.items():
        groups.setdefault((s % 2, size), []).append((s, page))
    for (odd, size), members in groups.items():
        here, first = section == members[0][0], members[0][1]
        for s, page in members[1:]:
            here = jnp.logical_or(here, section == s)
            first = jnp.where(section == s, page, first)

        @pl.when(here)
        def _():
            run(odd == 0, first, size * PAGE)


def forward_kernel(limits, w_in, w_out, vecs, *refs, state_in, plan, sizes_in, sizes_out):
    incoming = dict(zip(sizes_in, refs))
    refs = refs[len(sizes_in) + state_in :]
    outgoing = dict(zip(sizes_out, refs))
    state = refs[len(sizes_out) :]
    section = lax.axis_index("section")

    def run(is_attention, page, micro):
        size = micro // PAGE
        part = (limits, incoming.get(size), w_in, w_out, vecs, outgoing.get(size), *state)
        forward_part(*part, section, page, micro, is_attention)

    each_group(plan, section, run)


def forward_part(
    limits, incoming, w_in, w_out, vecs, y_ref, xin, out, sav, dh, br, probs_ref,
    section, page, micro, is_attention,
):
    width = xin.shape[1]
    group = micro // PAGE
    cross = jnp.where(section == 0, 1, 0)
    rows = pl.ds(pl.multiple_of(page * PAGE, PAGE), micro)

    def begin():
        x_low = xin[rows, :]
        if incoming is not None:
            x_low = jnp.where(section == 0, x_low, incoming[...])
        xin[rows, :] = x_low
        return x_low

    def finish(x_low, branch):
        br[rows, :] = branch
        gate, normed, inv = tail_parts(
            x_low.astype(F32), branch, gate_table(vecs, micro, width)
        )
        y = (normed * vecs[0:1, :] + vecs[1:2, :]).astype(BF16)
        if y_ref is not None:
            y_ref[...] = y
        out[rows, :] = y

    def attention():
        x_low = begin()
        x_text, x_visual = text_of(x_low), visual_of(x_low)

        for k in range(3):
            cols = block(k, width)
            sav[rows, cols] = to_pages(
                dot(x_visual, w_out[cols, :]).astype(BF16), dot(x_text, w_in[:, cols]).astype(BF16)
            )

        for i in range(group):
            here = page_rows(page, i)
            allowed = allowed_pairs(limits[pl.ds(page + i, 1), :], cross)
            pairs = width // (2 * HEAD_DIM)

            for first in range(0, pairs, TOGETHER):
                some = range(first, first + TOGETHER)
                scores = [
                    dot_nt(
                        sav[here, block(pairs + n, 128)],
                        stack_heads(sav[here, block(n, 128)]),
                    )
                    for n in some
                ]
                probs = [masked_softmax(one, allowed).astype(BF16) for one in scores]
                contexts = [
                    dot_tn(one, sav[here, block(2 * pairs + n, 128)])
                    for n, one in zip(some, probs)
                ]
                for n, one, context in zip(some, probs, contexts):
                    probs_ref[here, block(n, 2 * PAGE)] = one
                    sav[here, block(3 * pairs + n, 128)] = unstack_heads(context).astype(BF16)

        context = sav[rows, 3 * width :]
        finish(
            x_low,
            to_pages(
                dot(visual_of(context), w_out[3 * width :, :]),
                dot(text_of(context), w_in[:, 3 * width :]),
            ),
        )

    def feed():
        x_low = begin()

        hidden_width = w_in.shape[1]
        branch = None
        ahead = dot(x_low, w_in[:, :width])
        for start in range(0, hidden_width, width):
            cols = slice(start, start + width)
            hidden = ahead
            if start + width < hidden_width:
                ahead = dot(x_low, w_in[:, start + width : start + 2 * width])
            square = hidden * hidden
            tanh = jnp.tanh(hidden * (GELU_A + (GELU_A * GELU_B) * square))
            half = 0.5 + 0.5 * tanh
            active = hidden * half
            low = active.astype(BF16)
            sav[rows, cols] = low
            slope = half + (active * (1.0 - tanh)) * (
                GELU_A + (3.0 * GELU_A * GELU_B) * square
            )
            dh[rows, cols] = slope.astype(BF16)
            part = dot(low, w_out[cols, :])
            branch = part if branch is None else branch + part
        finish(x_low, branch)

    (attention if is_attention else feed)()


def backward_kernel(
    w_in, w_out, vecs, *refs, state_in, plan, sizes_in, sizes_out, sections, phase
):
    incoming = dict(zip(sizes_in, refs))
    late = phase == "rest"
    refs = refs[len(sizes_in) + late + state_in :]
    outgoing = dict(zip(sizes_out, refs))
    state, dc = refs[len(sizes_out) : -1 - late], refs[-1]
    if late:
        refs[-2][...] = jnp.zeros_like(refs[-2])
    section = lax.axis_index("section")

    def run(is_attention, page, micro):
        size = micro // PAGE
        part = (incoming.get(size), w_in, w_out, vecs, outgoing.get(size), *state, dc)
        backward_part(*part, section == sections - 1, page, micro, is_attention, phase)

    each_group(plan, section, run)


def backward_part(
    incoming, w_in, w_out, vecs, dx_ref, xin, out, sav, dh, br, probs_ref, grads, db, small, dc,
    is_last, page, micro, is_attention, phase,
):
    width = xin.shape[1]
    group = micro // PAGE
    rows = pl.ds(pl.multiple_of(page * PAGE, PAGE), micro)

    def tail():
        x = xin[rows, :].astype(F32)
        branch = br[rows, :]
        gate_rows = gate_table(vecs, micro, width)
        gate, normed, inv = tail_parts(x, branch, gate_rows)
        dy = grads[rows, :]
        if incoming is not None:
            dy = jnp.where(is_last, dy, incoming[...])
        dy = dy.astype(F32)
        dn = dy * vecs[0:1, :]
        du = inv * (
            dn
            - jnp.mean(dn, axis=-1, keepdims=True)
            - normed * jnp.mean(dn * normed, axis=-1, keepdims=True)
        )
        dbranch = (du * gate).astype(BF16)
        db[rows, :] = dbranch
        dz = jnp.sum(du * branch, axis=-1, keepdims=True) * gate * (1.0 - gate)
        weighted = dz * x
        sums = jnp.concatenate(
            [
                jnp.sum(dy * normed, axis=0, keepdims=True),
                jnp.sum(dy, axis=0, keepdims=True),
                jnp.sum(text_of(weighted), axis=0, keepdims=True),
                jnp.sum(visual_of(weighted), axis=0, keepdims=True),
                jnp.zeros((4, width), F32),
            ],
            axis=0,
        )
        small[pl.ds(pl.multiple_of(page * 8, 8), 8), :] = sums
        for i in range(1, group):
            small[pl.ds(pl.multiple_of((page + i) * 8, 8), 8), :] = jnp.zeros_like(sums)
        br[rows, :] = du + dz * gate_rows

    def finish(total):
        dx = total.astype(BF16)
        if dx_ref is not None:
            dx_ref[...] = dx
        grads[rows, :] = dx

    def attention():
        if phase != "rest":
            tail()
        if phase == "tail":
            return
        dbranch = db[rows, :]
        dc[:micro, :] = to_pages(
            dot_nt(visual_of(dbranch), w_out[3 * width :, :]).astype(BF16),
            dot_nt(text_of(dbranch), w_in[:, 3 * width :]).astype(BF16),
        )
        for i in range(group):
            here = page_rows(page, i)
            own = slice(i * PAGE, (i + 1) * PAGE)
            pairs = width // (2 * HEAD_DIM)

            for first in range(0, pairs, TOGETHER):
                some = range(first, first + TOGETHER)
                contexts = [stack_heads(dc[own, block(n, 128)]) for n in some]
                dprobs = [
                    dot_nt(sav[here, block(2 * pairs + n, 128)], one)
                    for n, one in zip(some, contexts)
                ]
                low = [probs_ref[here, block(n, 2 * PAGE)] for n in some]
                dvalues = [dot(one, context) for one, context in zip(low, contexts)]
                dscores = []
                for one, change in zip(low, dprobs):
                    probs = one.astype(F32)
                    mean = jnp.sum(change * probs, axis=0, keepdims=True)
                    dscores.append((probs * (change - mean)).astype(BF16))
                dkeys = [
                    dot(one, stack_heads(sav[here, block(n, 128)]))
                    for n, one in zip(some, dscores)
                ]
                dqueries = [
                    dot_tn(one, sav[here, block(pairs + n, 128)])
                    for n, one in zip(some, dscores)
                ]
                for n, dquery, dkey, dvalue in zip(some, dqueries, dkeys, dvalues):
                    dh[here, block(2 * pairs + n, 128)] = dvalue.astype(BF16)
                    dh[here, block(pairs + n, 128)] = (dkey * SCORE_SCALE).astype(BF16)
                    dh[here, block(n, 128)] = (unstack_heads(dquery) * SCORE_SCALE).astype(BF16)

        text, visual = None, None
        for k in range(3):
            cols = slice(k * width, (k + 1) * width)
            part = dh[rows, cols]
            one = dot_nt(text_of(part), w_in[:, cols])
            two = dot_nt(visual_of(part), w_out[cols, :])
            text = one if text is None else text + one
            visual = two if visual is None else visual + two
        finish(br[rows, :] + to_pages(visual, text))

    def feed():
        if phase != "rest":
            tail()
        if phase == "tail":
            return
        dbranch, total = db[rows, :], br[rows, :]
        for start in range(0, w_in.shape[1], width):
            cols = slice(start, start + width)
            dhidden = (dot_nt(dbranch, w_out[cols, :]) * dh[rows, cols].astype(F32)).astype(BF16)
            dh[rows, cols] = dhidden
            total = total + dot_nt(dhidden, w_in[:, cols])
        finish(total)

    (attention if is_attention else feed)()


def weight_chunk(kind, core, xin, sav, dh, db, own_ref, other_ref, chunk):
    part, width = own_ref.shape
    start = chunk * part
    cols = slice(start, start + part)

    def put(grad_a, grad_b):
        low_a = jnp.concatenate(
            [grad_a[i : i + part].astype(BF16) for i in range(0, width, part)], axis=1
        )
        low_b = grad_b.astype(BF16)
        own_ref[...] = jnp.where(core == 0, low_a, low_b)
        other_ref[...] = jnp.where(core == 0, low_b, low_a)

    @pl.when(kind == 1)
    def attention():
        block, inner = start // width, start % width
        inner_cols = slice(inner, inner + part)
        if block < 3:
            left, right = xin[...], dh[:, block * width : (block + 1) * width]
            put(
                dot_tn(text_of(left), text_of(dh[:, cols])),
                dot_tn(visual_of(left[:, inner_cols]), visual_of(right)),
            )
        else:
            left, right = sav[:, 3 * width :], db[...]
            put(
                dot_tn(text_of(left), text_of(right[:, inner_cols])),
                dot_tn(visual_of(left[:, inner_cols]), visual_of(right)),
            )

    @pl.when(kind == 2)
    def feed():
        put(dot_tn(xin[...], dh[:, cols]), dot_tn(sav[:, cols], db[...]))


def work_kernel(*refs, chunk, place, placed, flush):
    refs = list(refs)
    del refs[0]
    core = lax.axis_index("dp") % 2

    def take(count):
        taken = refs[:count]
        del refs[:count]
        return taken

    factors = take(4) if chunk is not None else None
    rows_in = take(flush)
    if place is not None:
        own, other = take(2)
        take(placed)
    partial = take(2) if chunk is not None else None
    rows_out = take(flush)
    if place is not None:
        grad_in, grad_out = take(2)
    (token,) = take(1)
    token[...] = jnp.zeros_like(token)
    copies = []
    if flush:
        row_sems = refs.pop()
        for i, (source, target) in enumerate(zip(rows_in, rows_out)):
            copies.append(pltpu.make_async_copy(source, target, row_sems.at[i]))
            copies[-1].start()
    if place is not None:
        buf_a, buf_b, sems = refs
        part, width = buf_b.shape
        start = place * part
        mine, theirs = own[...], other[...]
        buf_b[...] = jnp.where(core == 0, theirs, mine).astype(F32)
        copies.append(
            pltpu.make_async_copy(buf_b, grad_out.at[pl.ds(start, part), :], sems.at[0])
        )
        copies[-1].start()
        for i in range(width // part):
            cols = slice(i * part, (i + 1) * part)
            buf_a[cols, :] = jnp.where(core == 0, mine[:, cols], theirs[:, cols]).astype(F32)
        copies.append(
            pltpu.make_async_copy(buf_a, grad_in.at[:, pl.ds(start, part)], sems.at[1])
        )
        copies[-1].start()
    if chunk is not None:
        kind = 1 + lax.axis_index("section") % 2
        weight_chunk(kind, core, *factors, *partial, chunk)
    for copy in copies:
        copy.wait()


def add_low(a, b):
    return (a.astype(F32) + b.astype(F32)).astype(BF16)


def outer_kernel(*refs, new, total):
    refs = list(refs)
    del refs[0]
    chip = lax.axis_index("dp") // 2
    new_in = [refs.pop(0)[...] for _ in range(2 * new)]
    total_in = [refs.pop(0)[...] for _ in range(2 * total)]
    values = []
    if new:
        values.append(add_low(*new_in))
        refs.pop(0)[...] = values[-1]
    if total:
        values.append(add_low(*total_in))
        refs.pop(0)[...] = values[-1]
    if new and total:
        middle = jnp.logical_or(chip == 1, chip == 2)
        refs.pop(0)[...] = jnp.where(middle, values[1], values[0])
    token = refs.pop(0)
    token[...] = jnp.zeros_like(token)


def inner_kernel(*refs, inner, final):
    refs = list(refs)
    del refs[0]
    chip = lax.axis_index("dp") // 2
    got = refs.pop(0)[...]
    first = refs.pop(0)[...] if inner else None
    total = refs.pop(0)[...] if final else None
    if inner:
        refs.pop(0)[...] = add_low(first, got)
    if final:
        middle = jnp.logical_or(chip == 1, chip == 2)
        refs.pop(0)[...] = jnp.where(middle, total, got)
    token = refs.pop(0)
    token[...] = jnp.zeros_like(token)


def sum_pages_kernel(token_in, small, total_ref, token):
    total = small[0:8, :]
    for i in range(8, small.shape[0], 8):
        total += small[i : i + 8, :]
    total_ref[...] = total
    token[...] = jnp.zeros_like(token)


def add_kernel(token_in, a, b, *refs):
    total = a[...] + b[...]
    *outs, token = refs
    token[...] = jnp.zeros_like(token)
    if len(outs) == 1:
        outs[0][...] = total
    else:
        gain, bias, gates = outs
        gain[...] = total[0:1]
        bias[...] = total[1:2]
        gates[...] = total[2:4]


def struct(shape, dtype):
    return jax.ShapeDtypeStruct(shape, dtype)


def params(mebibytes):
    return pltpu.CompilerParams(vmem_limit_bytes=mebibytes << 20)


def in_vmem(*arrays):
    return [pltpu.with_memory_space_constraint(a, pltpu.VMEM) for a in arrays]


def run_load(gain, bias, gates, counts, *arrays):
    width = gain.shape[1]
    inputs = [*arrays, gain, bias, gates, counts.T]
    return pl.pallas_call(
        functools.partial(load_kernel, count=len(arrays)),
        out_shape=[struct((8, width), F32), struct((counts.shape[0], 4 * PAGE), jnp.int32)]
        + [pltpu.VMEM(a.shape, a.dtype) for a in arrays],
        in_specs=[HBM] * len(inputs),
        out_specs=[VMEM] * (2 + len(arrays)),
        scratch_shapes=[
            pltpu.VMEM((1, width), F32),
            pltpu.VMEM((1, width), F32),
            pltpu.VMEM((2, width), F32),
            pltpu.SMEM((2, counts.shape[0]), jnp.int32),
            pltpu.SemaphoreType.DMA((len(inputs),)),
        ],
        compiler_params=params(4),
        name="load_weights",
    )(*[pltpu.with_memory_space_constraint(a, pltpu.HBM) for a in inputs])


def run_forward(plan, limits, incoming, sizes_out, w_in, w_out, vecs, state):
    rows, width = state[0].shape
    hidden = w_in.shape[1]
    sizes_in = tuple(incoming)
    first = 4 + len(sizes_in)
    got = pl.pallas_call(
        functools.partial(
            forward_kernel,
            state_in=len(state), plan=plan, sizes_in=sizes_in, sizes_out=sizes_out,
        ),
        out_shape=[struct((size * PAGE, width), BF16) for size in sizes_out]
        + [
            pltpu.VMEM((rows, width), BF16),
            pltpu.VMEM((rows, width), BF16),
            pltpu.VMEM((rows, hidden), BF16),
            pltpu.VMEM((rows, hidden), BF16),
            pltpu.VMEM((rows, width), F32),
            pltpu.VMEM((rows, 2 * PAGE * (width // (2 * HEAD_DIM))), BF16),
        ],
        in_specs=[VMEM] * (first + len(state)),
        out_specs=[VMEM] * (len(sizes_out) + 6),
        input_output_aliases={first + i: len(sizes_out) + i for i in range(len(state))},
        compiler_params=params(12),
        name="forward_pages",
    )(limits, *in_vmem(w_in, w_out), vecs, *incoming.values(), *state)
    return dict(zip(sizes_out, got)), got[len(sizes_out) :]


def run_backward(
    plan, incoming, sizes_out, sections, w_in, w_out, vecs, state, back, phase=None, token=None
):
    rows, width = back[0].shape
    every = list(state) + list(back)
    sizes_in = tuple(incoming)
    late = [] if token is None else [token]
    first = 3 + len(sizes_in) + len(late)
    largest = max(size for _, size in plan.values())
    got = pl.pallas_call(
        functools.partial(
            backward_kernel,
            state_in=len(every), plan=plan, sizes_in=sizes_in, sizes_out=sizes_out,
            sections=sections, phase=phase,
        ),
        out_shape=[struct((size * PAGE, width), BF16) for size in sizes_out]
        + [pltpu.VMEM(s.shape, s.dtype) for s in state]
        + [
            pltpu.VMEM((rows, width), BF16),
            pltpu.VMEM((rows, width), BF16),
            pltpu.VMEM((8 * rows // PAGE, width), F32),
        ]
        + [struct(TOKEN, F32) for _ in late],
        in_specs=[VMEM] * (first + len(every)),
        out_specs=[VMEM] * (len(sizes_out) + 9 + len(late)),
        input_output_aliases={first + i: len(sizes_out) + i for i in range(len(every))},
        scratch_shapes=[pltpu.VMEM((largest * PAGE, width), BF16)],
        compiler_params=params(12),
        name="backward_pages",
    )(*in_vmem(w_in, w_out), vecs, *incoming.values(), *late, *every)
    state_out = got[len(sizes_out) :]
    return dict(zip(sizes_out, got)), state_out[:6], state_out[6:9], *state_out[9:]


def send_pages(values, plan, step, sections):
    sent = {}
    for size, value in values.items():
        pairs = [
            (s, s + step)
            for s, (_, own) in plan.items()
            if own == size and 0 <= s + step < sections
        ]
        sent[size] = lax.ppermute(value, "section", pairs)
    return sent


def micro_batches(sizes, pages):
    if sum(sizes) != pages:
        sizes = (1,) * pages
    starts = [sum(sizes[:i]) for i in range(len(sizes))]
    return list(zip(starts, sizes))


TOKEN = (8, 128)


def run_work(token, factors, chunk, totals, place, grads, flush=()):
    width = factors[0].shape[1]
    hidden = factors[1].shape[1]
    part = hidden // CHUNKS
    inputs, specs = [token], [VMEM]
    outs, out_specs, scratch, aliases = [], [], [], {}
    if chunk is not None:
        inputs += in_vmem(*factors)
        specs += [VMEM] * 4
        outs += [struct((part, width), BF16)] * 2
        out_specs += [VMEM] * 2
    if flush:
        inputs += in_vmem(*flush)
        specs += [VMEM] * len(flush)
        outs += [pltpu.HBM(a.shape, a.dtype) for a in flush]
        out_specs += [HBM] * len(flush)
    if place is not None:
        inputs += list(totals)
        specs += [VMEM] * 2
        aliases = {len(inputs) + i: len(outs) + i for i in range(len(grads))}
        inputs += list(grads)
        specs += [HBM] * len(grads)
        outs += [pltpu.HBM((width, hidden), F32), pltpu.HBM((hidden, width), F32)]
        out_specs += [HBM] * 2
        scratch = [
            pltpu.VMEM((width, part), F32),
            pltpu.VMEM((part, width), F32),
            pltpu.SemaphoreType.DMA((2,)),
        ]
    if flush:
        scratch.append(pltpu.SemaphoreType.DMA((len(flush),)))
    *got, token = pl.pallas_call(
        functools.partial(
            work_kernel, chunk=chunk, place=place, placed=len(grads), flush=len(flush)
        ),
        out_shape=outs + [struct(TOKEN, F32)],
        in_specs=specs,
        out_specs=out_specs + [VMEM],
        input_output_aliases=aliases,
        scratch_shapes=scratch,
        compiler_params=params(16),
        name="work_beside",
    )(*inputs)
    made = [got.pop(0) for _ in range(2)] if chunk is not None else None
    flushed = [got.pop(0) for _ in flush]
    return made, (got if place is not None else grads), flushed, token


def run_step(kernel, name, inputs, outs):
    return pl.pallas_call(
        kernel,
        out_shape=[struct(inputs[-1].shape, inputs[-1].dtype)] * outs + [struct(TOKEN, F32)],
        in_specs=[VMEM] * len(inputs),
        out_specs=[VMEM] * (outs + 1),
        compiler_params=params(8),
        name=name,
    )(*inputs)


class SmallSum:
    def __init__(self, small):
        self.small = small
        self.size = lax.axis_size("dp")
        self.step = 0
        self.total = None
        self.got = None

    def advance(self, token):
        if self.step == 0:
            self.total, token = pl.pallas_call(
                sum_pages_kernel,
                out_shape=[struct((8, self.small.shape[1]), F32), struct(TOKEN, F32)],
                in_specs=[VMEM, VMEM],
                out_specs=[VMEM, VMEM],
                compiler_params=params(4),
                name="small_sum",
            )(token, *in_vmem(self.small))
            self.step = 1
        elif self.got is not None:
            width = self.total.shape[1]
            heights = (8,) if self.step < self.size else (1, 1, 2)
            *outs, token = pl.pallas_call(
                add_kernel,
                out_shape=[struct((h, width), F32) for h in heights] + [struct(TOKEN, F32)],
                in_specs=[VMEM] * 3,
                out_specs=[VMEM] * (len(heights) + 1),
                compiler_params=params(4),
                name="small_sum",
            )(token, self.total, self.got)
            self.total = outs[0] if len(heights) == 1 else outs
            self.got = None
        if self.step < self.size:
            pairs = [(i, i ^ self.step) for i in range(self.size)]
            self.got = lax.ppermute(self.total, "dp", pairs)
            self.step *= 2
        return token

    def done(self):
        return self.step >= self.size and self.got is None


def sum_over_line(token, factors, late):
    count = CHUNKS
    order = [(k + count * 3 // 4) % count for k in range(count)]
    small, flush = None, ()
    swap = [(i, i ^ 1) for i in range(8)]
    outer = [(i, i ^ 2) for i in range(8)]
    middle = [(2, 4), (3, 5), (4, 2), (5, 3)]
    lag = LAG
    made, firsts, inners, totals, finals = {}, {}, {}, {}, {}
    got_outer, got_inner = {}, {}
    grads, flushed = (), None

    def work(token, grads, chunk, place, flush=()):
        chunk = chunk if chunk is not None and chunk < count else None
        place = place if place is not None and 0 <= place < count else None
        if chunk is None and place is None:
            return token, grads, ()
        pair = finals.pop(place) if place is not None else None
        new, grads, flushed, token = run_work(
            token,
            factors,
            None if chunk is None else order[chunk],
            pair,
            None if place is None else order[place],
            grads,
            flush,
        )
        if new:
            made[chunk] = (new[0], lax.ppermute(new[1], "dp", swap))
        return token, grads, flushed

    for k in range(AHEAD):
        token, grads, _ = work(token, grads, k, None)

    def at(half, stage):
        k, odd = divmod(half - stage * lag, 2)
        return k if not odd and 0 <= k < count else None

    for half in range(2 * count - 1 + 3 * lag):
        if half % 2 == 0:
            new, total = at(half, 0), at(half, 2)
            inputs = [token]
            if new is not None:
                inputs += made.pop(new)
            if total is not None:
                inputs += [inners.pop(total), got_inner.pop(half - lag)]
            if len(inputs) > 1:
                both = new is not None and total is not None
                kernel = functools.partial(
                    outer_kernel, new=int(new is not None), total=int(total is not None)
                )
                *outs, token = run_step(kernel, "outer_step", inputs, 2 + 1 if both else 1)
                send = outs[-1]
                if new is not None:
                    firsts[new] = outs[0]
                if total is not None:
                    totals[total] = outs[1 if both else 0]
                got_outer[half] = lax.ppermute(send, "dp", outer)
            elif at(half - 1, 3) is not None:
                token, grads, _ = work(token, grads, None, at(half - 1, 3))
            if half == 2:
                (factors, flush, rows), token = late(token)
                small = SmallSum(rows)
                for k in range(AHEAD + 1, AHEAD + 1 + EARLY):
                    token, grads, rows = work(token, grads, k, None, flush)
                    flush, flushed = (), rows or flushed
            if half >= 4 and half % 4 == 0 and not small.done():
                token = small.advance(token)
        else:
            inner, final = at(half, 1), at(half, 3)
            if inner is not None or final is not None:
                inputs = [token, got_outer.pop(half - lag)]
                if inner is not None:
                    inputs.append(firsts.pop(inner))
                if final is not None:
                    inputs.append(totals.pop(final))
                kernel = functools.partial(
                    inner_kernel, inner=inner is not None, final=final is not None
                )
                *outs, token = run_step(
                    kernel, "inner_step", inputs, (inner is not None) + (final is not None)
                )
                if inner is not None:
                    inners[inner] = outs[0]
                    got_inner[half] = lax.ppermute(outs[0], "dp", middle)
                if final is not None:
                    finals[final] = (outs[-1], lax.ppermute(outs[-1], "dp", swap))
            chunk = (half - 1) // 2 + AHEAD + (EARLY if half > 1 else 0)
            place = at(half - 2, 3)
            token, grads, _ = work(token, grads, chunk, place if place in finals else None)
    token, grads, _ = work(token, grads, None, count - 1)
    while not small.done():
        token = small.advance(token)
    return grads, flushed, small


def body(acts, cotan, counts, weight_in, weight_out, ln_gain, ln_bias, gate_vec):
    sections = lax.axis_size("section")
    dp_index = lax.axis_index("dp")
    dp_size = lax.axis_size("dp")
    rows, width = acts.shape
    vecs, limits, w_in, w_out, acts, cotan = run_load(
        ln_gain, ln_bias, gate_vec[0], counts, weight_in[0], weight_out[0], acts, cotan
    )
    core = dp_index % 2
    ahead = micro_batches(FORWARD, rows // PAGE)
    behind = micro_batches(BACKWARD, rows // PAGE)
    last = sections - 1
    state, back = (acts,), (cotan,)
    incoming, upstream = {}, {}
    slot, tick = 0, 0
    while slot < len(behind) + BACK_LAG * last:
        plan = {s: ahead[tick - s] for s in range(sections) if 0 <= tick - s < len(ahead)}
        if plan:
            sizes = tuple(sorted({size for s, (_, size) in plan.items() if s < last}))
            values, state = run_forward(
                plan, limits, incoming, sizes, w_in, w_out, vecs, state
            )
            incoming = send_pages(values, plan, 1, sections)
        tick += 1
        done = sum(size for _, size in ahead[: max(tick - last, 0)])
        if slot < len(behind) and sum(behind[slot]) > done:
            continue
        plan = {
            s: behind[slot - BACK_LAG * (last - s)]
            for s in range(sections)
            if 0 <= slot - BACK_LAG * (last - s) < len(behind)
        }
        sizes = tuple(sorted({size for s, (_, size) in plan.items() if s > 0}))
        final = slot == len(behind) + BACK_LAG * last - 1
        values, state, back = run_backward(
            plan, upstream.pop(slot, {}), sizes, sections, w_in, w_out, vecs, state, back,
            phase="tail" if final else None,
        )
        upstream[slot + BACK_LAG] = send_pages(values, plan, -1, sections)
        slot += 1

    def parts(state, back):
        return (state[0], state[2], state[3], back[1]), (state[1], back[0]), back[2]

    def late(token):
        _, *both, token = run_backward(
            plan, {}, (), sections, w_in, w_out, vecs, state, back, phase="rest", token=token
        )
        return parts(*both), token

    token = jnp.zeros(TOKEN, F32)
    if dp_size == 8:
        (grad_in, grad_out), (outputs, grads), small = sum_over_line(
            token, parts(state, back)[0], late
        )
    else:
        (factors, (outputs, grads), small), token = late(token)
        small = SmallSum(small)
        so_far = ()
        for k in range(CHUNKS):
            (own, other), _, _, token = run_work(token, factors, k, None, None, ())
            pair = jnp.where(core == 0, jnp.stack([own, other]), jnp.stack([other, own]))
            pair = lax.psum(pair, "dp")
            pair = jnp.where(core == 0, pair, pair[::-1])
            _, so_far, _, token = run_work(
                token, factors, None, (pair[0], pair[1]), k, so_far
            )
        grad_in, grad_out = so_far
        while not small.done():
            token = small.advance(token)
    grad_gain, grad_bias, grad_gate = small.total
    return (
        outputs[None],
        grads[None],
        grad_in[None],
        grad_out[None],
        grad_gain,
        grad_bias,
        grad_gate[None],
    )


def solution(mesh):
    return jax.shard_map(
        body,
        mesh=mesh,
        in_specs=(
            P("dp", None),
            P("dp", None),
            P("dp", None),
            P("section", None, None),
            P("section", None, None),
            P("section", None),
            P("section", None),
            P("section", None, None),
        ),
        out_specs=(
            P("section", "dp", None),
            P("section", "dp", None),
            P("section", None, None),
            P("section", None, None),
            P("section", None),
            P("section", None),
            P("section", None, None),
        ),
        check_vma=False,
    )
```
